32 devices in a mesh: dp: 16 (over z, y, core), seq: 2 (over x).
Axes of the slice: x: 2, y: 2, z: 4, core: 2. Of those that a mesh axis runs over, the one named last changes fastest.
Arguments:
- frames: bfloat16 [32, 1536, 1024], P('dp', 'seq'), may hold values from -6 to 6
- segments: int32 [32, 1536], P('dp', 'seq'), may hold values from 0 to 3, as said below
- text_states: bfloat16 [32, 4, 64, 768], P('dp'), may hold values from -6 to 6
- text_lengths: int32 [32, 4], P('dp'), may hold values from 1 to 64, as said below
- cotangent: bfloat16 [32, 1536, 1024], P('dp', 'seq'), may hold values from -6 to 6
- self_norm_gain: bfloat16 [1024], P(('dp', 'seq')), may hold values from 0.25 to 1.75
- self_norm_bias: bfloat16 [1024], P(('dp', 'seq')), may hold values from -3 to 3
- self_qkv: bfloat16 [1024, 3072], P(('dp', 'seq')), may hold values from -0.1875 to 0.1875
- self_output: bfloat16 [1024, 1024], P(('dp', 'seq')), may hold values from -0.75 to 0.75
- cross_norm_gain: bfloat16 [1024], P(('dp', 'seq')), may hold values from 0.25 to 1.75
- cross_norm_bias: bfloat16 [1024], P(('dp', 'seq')), may hold values from -3 to 3
- cross_query: bfloat16 [1024, 1024], P(('dp', 'seq')), may hold values from -0.1875 to 0.1875
- text_project: bfloat16 [768, 1024], P(('dp', 'seq')), may hold values from -0.21875 to 0.21875
- text_bias: bfloat16 [1024], P(('dp', 'seq')), may hold values from -3 to 3
- cross_keyvalue: bfloat16 [1024, 2048], P(('dp', 'seq')), may hold values from -0.1875 to 0.1875
- cross_output: bfloat16 [1024, 1024], P(('dp', 'seq')), may hold values from -0.375 to 0.375
- feed_norm_gain: bfloat16 [1024], P(('dp', 'seq')), may hold values from 0.25 to 1.75
- feed_norm_bias: bfloat16 [1024], P(('dp', 'seq')), may hold values from -3 to 3
- feed_in: bfloat16 [1024, 4096], P(('dp', 'seq')), may hold values from -0.1875 to 0.1875
- feed_out: bfloat16 [4096, 1024], P(('dp', 'seq')), may hold values from -0.09375 to 0.09375
Outputs:
- block_out: bfloat16 [32, 1536, 1024], P('dp', 'seq')
- frames_grad: bfloat16 [32, 1536, 1024], P('dp', 'seq')
- text_grad: float32 [32, 4, 64, 768], P('dp', None, 'seq')
- self_norm_gain_grad: float32 [1024], P(('dp', 'seq'))
- self_norm_bias_grad: float32 [1024], P(('dp', 'seq'))
- self_qkv_grad: float32 [1024, 3072], P(('dp', 'seq'))
- self_output_grad: float32 [1024, 1024], P(('dp', 'seq'))
- cross_norm_gain_grad: float32 [1024], P(('dp', 'seq'))
- cross_norm_bias_grad: float32 [1024], P(('dp', 'seq'))
- cross_query_grad: float32 [1024, 1024], P(('dp', 'seq'))
- text_project_grad: float32 [768, 1024], P(('dp', 'seq'))
- text_bias_grad: float32 [1024], P(('dp', 'seq'))
- cross_keyvalue_grad: float32 [1024, 2048], P(('dp', 'seq'))
- cross_output_grad: float32 [1024, 1024], P(('dp', 'seq'))
- feed_norm_gain_grad: float32 [1024], P(('dp', 'seq'))
- feed_norm_bias_grad: float32 [1024], P(('dp', 'seq'))
- feed_in_grad: float32 [1024, 4096], P(('dp', 'seq'))
- feed_out_grad: float32 [4096, 1024], P(('dp', 'seq'))
The draws below stay inside these ranges and needn't reach their ends.
Inputs may be any that keep to these rules, and one draw needn't show every extreme that they name: `segments`: each row is cut into consecutive clips numbered from 0 upward; ids never fall along a row. Slots of clip m of a row at or beyond text_lengths[row, m] are padding.
All inputs are finite; a program needn't handle non-finite values.
Results may differ from the reference program's by a relative error of at most 0.035.
Values may be sent and summed in bfloat16 or wider, within the bound.
A program may use at most 576 MiB of HBM per device.

```python
import math
import jax
import jax.numpy as jnp
from jax import lax

D = 1024
HEADS = 16
HD = 64
FF = 4096
TD = 768
TXT = 64
SEGS = 4
ROW_LEN = 1536
ROWS_DEV = 2
ROWS = 32


def draw_segments(key, part):
    key = jax.random.fold_in(key, 11)
    keys = jax.random.split(key, 5)
    group_count = ROWS // ROWS_DEV
    tail = jax.random.randint(keys[0], (ROWS, 1), 1, ROW_LEN // 32 + 1)
    reach = ROW_LEN // 12
    first = ROW_LEN // 3 + jax.random.randint(keys[1], (ROWS, 1), -reach, reach + 1)
    second = 2 * ROW_LEN // 3 + jax.random.randint(keys[2], (ROWS, 1), -reach, reach + 1)
    random_long = jax.random.randint(keys[3], (ROWS, 1), 0, 2)
    chosen = jax.random.randint(keys[4], (group_count, 1), 0, ROWS_DEV)
    columns = jnp.arange(ROWS_DEV, dtype=jnp.int32)[None, :]
    forced_long = (columns == chosen).astype(jnp.int32).reshape(ROWS, 1)
    forced_short = (columns == (chosen + 1) % ROWS_DEV).astype(jnp.int32).reshape(ROWS, 1)
    long_rows = jnp.maximum(random_long, forced_long) * (1 - forced_short)
    last = ROW_LEN - tail
    cut_one = jnp.where(long_rows == 1, last, first)
    cut_two = jnp.where(long_rows == 1, ROW_LEN, second)
    cut_three = jnp.where(long_rows == 1, ROW_LEN, last)
    positions = jnp.arange(ROW_LEN, dtype=jnp.int32)[None, :]
    ids = (positions >= cut_one).astype(jnp.int32) + (positions >= cut_two).astype(jnp.int32)
    return ids + (positions >= cut_three).astype(jnp.int32)


def draw_text_lengths(key, part):
    key = jax.random.fold_in(key, 23)
    keys = jax.random.split(key, 2)
    lengths = jax.random.randint(keys[0], (ROWS, SEGS), 1, TXT + 1)
    spot = jax.random.randint(keys[1], (ROWS, 1), 0, SEGS)
    columns = jnp.arange(SEGS, dtype=jnp.int32)[None, :]
    rows_index = jnp.arange(ROWS, dtype=jnp.int32)[:, None]
    lengths = jnp.where(columns == spot, TXT, lengths)
    return jnp.where((rows_index == 0) & (columns == (spot + 1) % SEGS), 1, lengths)


def block_scale(stream_key, dims, cuts, least, top_value):
    loudness = 1.0
    for position, shards_of in cuts:
        heights = jax.random.uniform(jax.random.fold_in(jax.random.fold_in(stream_key, 6), position), (shards_of,), jnp.float32, least / len(cuts), top_value / len(cuts))
        loudness = loudness * jnp.repeat(jnp.exp(heights), dims[position] // shards_of).reshape((-1,) + (1,) * (len(dims) - 1 - position))
    return loudness


def bell_draw(rng, dims, scale, limit, shards=(), kind=jnp.bfloat16):
    array = jax.random.normal(rng, dims, jnp.float32) * scale
    if len(shards) > 0:
        array = block_scale(rng, dims, shards, -0.22, 0.18) * array
    return jnp.clip(array, min=-limit, max=limit).astype(kind)


def setup_inputs(seed: int = 0) -> dict:
    arg_keys = jax.random.split(jax.random.key(seed), 21)
    return {
        "frames": bell_draw(arg_keys[0], (ROWS, ROW_LEN, D), 1.0, 6.0, ((0, 16), (1, 2))),
        "segments": draw_segments(jax.random.fold_in(arg_keys[20], 71), 0),
        "text_states": bell_draw(arg_keys[2], (ROWS, SEGS, TXT, TD), 1.0, 6.0, ((0, 16),)),
        "text_lengths": draw_text_lengths(jax.random.fold_in(arg_keys[20], 71), 0),
        "cotangent": bell_draw(arg_keys[4], (ROWS, ROW_LEN, D), 1.0, 6.0, ((0, 16), (1, 2))),
        "self_norm_gain": jnp.clip(1.0 + 0.15 * jax.random.normal(arg_keys[5], (D,), jnp.float32), 0.25, 1.75).astype(jnp.bfloat16),
        "self_norm_bias": bell_draw(arg_keys[6], (D,), 0.3, 3.0, ((0, 32),)),
        "self_qkv": bell_draw(arg_keys[7], (D, 3 * D), D ** -0.5, 0.1875, ((0, 32),)),
        "self_output": bell_draw(arg_keys[8], (D, D), (D // 16) ** -0.5, 0.75, ((0, 32),)),
        "cross_norm_gain": jnp.clip(1.0 + 0.15 * jax.random.normal(arg_keys[9], (D,), jnp.float32), 0.25, 1.75).astype(jnp.bfloat16),
        "cross_norm_bias": bell_draw(arg_keys[10], (D,), 0.3, 3.0, ((0, 32),)),
        "cross_query": bell_draw(arg_keys[11], (D, D), D ** -0.5, 0.1875, ((0, 32),)),
        "text_project": bell_draw(arg_keys[12], (TD, D), TD ** -0.5, 0.21875, ((0, 32),)),
        "text_bias": bell_draw(arg_keys[13], (D,), 0.3, 3.0, ((0, 32),)),
        "cross_keyvalue": bell_draw(arg_keys[14], (D, 2 * D), D ** -0.5, 0.1875, ((0, 32),)),
        "cross_output": bell_draw(arg_keys[15], (D, D), (D // 4) ** -0.5, 0.375, ((0, 32),)),
        "feed_norm_gain": jnp.clip(1.0 + 0.15 * jax.random.normal(arg_keys[16], (D,), jnp.float32), 0.25, 1.75).astype(jnp.bfloat16),
        "feed_norm_bias": bell_draw(arg_keys[17], (D,), 0.3, 3.0, ((0, 32),)),
        "feed_in": bell_draw(arg_keys[18], (D, FF), D ** -0.5, 0.1875, ((0, 32),)),
        "feed_out": bell_draw(arg_keys[19], (FF, D), FF ** -0.5, 0.09375, ((0, 32),)),
    }


@jax.custom_vjp
def low(v):
    return lax.optimization_barrier(v.astype(jnp.bfloat16)).astype(jnp.float32)

@jax.custom_vjp
def low_back(v):
    return v

def low_keep(v):
    return (low(v), None)

def low_pass(kept, grad):
    return (grad,)

def back_keep(v):
    return (v, None)

def back_low(kept, grad):
    return (low(grad),)
low.defvjp(low_keep, low_pass)
low_back.defvjp(back_keep, back_low)
epsilon = 1e-05
big_negative = -1e+30
highest = lax.Precision.HIGHEST

def layer_norm(values, gain, shift):
    centre = lax.optimization_barrier(jnp.mean(values, axis=-1, keepdims=True))
    centred = values - centre
    spread = lax.optimization_barrier(jnp.mean(centred * centred, axis=-1, keepdims=True))
    return centred * lax.rsqrt(spread + epsilon) * gain + shift

def matmul(left, right):
    return jnp.dot(left, right, preferred_element_type=jnp.float32, precision=highest)

def masked_softmax(scores, allowed):
    masked = jnp.where(allowed, scores, big_negative)
    maximum = lax.optimization_barrier(jnp.max(masked, axis=-1, keepdims=True))
    weights = jnp.where(allowed, jnp.exp(masked - maximum), 0.0)
    return weights / lax.optimization_barrier(jnp.sum(weights, axis=-1, keepdims=True))

def self_attention(queries, keys, values, segment_row):
    block = math.gcd(ROW_LEN, 512)
    scale = HD ** (-0.5)
    positions = jnp.arange(ROW_LEN, dtype=jnp.int32)

    def one_block(start):
        query_block = lax.dynamic_slice_in_dim(queries, start, block, 0)
        query_segments = lax.dynamic_slice_in_dim(segment_row, start, block, 0)
        query_positions = start + jnp.arange(block, dtype=jnp.int32)
        scores = low_back(jnp.einsum('qhd,khd->hqk', query_block, keys, precision=highest) * scale)
        allowed = (positions[None, :] <= query_positions[:, None]) & (segment_row[None, :] == query_segments[:, None])
        probs = low(masked_softmax(scores, allowed[None]))
        return jnp.einsum('hqk,khd->qhd', probs, values, precision=highest)
    starts = (jnp.arange(ROW_LEN // block) * block).astype(jnp.int32)
    outputs = lax.map(jax.checkpoint(one_block), starts)
    return outputs.reshape(ROW_LEN, D)

def cross_attention(queries, keys, values, segment_row, length_row):
    scale = HD ** (-0.5)
    slots = jnp.arange(SEGS * TXT, dtype=jnp.int32)
    key_clip = slots // TXT
    key_slot = slots % TXT
    live = key_slot < jnp.repeat(length_row, TXT)
    allowed = (segment_row[:, None] == key_clip[None, :]) & live[None, :]
    scores = low_back(jnp.einsum('qhd,khd->hqk', queries, keys, precision=highest) * scale)
    probs = low(masked_softmax(scores, allowed[None]))
    return jnp.einsum('hqk,khd->qhd', probs, values, precision=highest).reshape(ROW_LEN, D)

def row_forward(inputs, segment_row, text_row, length_row, params):
    gain_one, shift_one, qkv_full, out_full, gain_two, shift_two, query_full, project_full, bias_full, keyvalue_full, crossout_full, gain_three, shift_three, feedin_full, feedout_full = params
    normed_one = low(layer_norm(inputs, gain_one, shift_one))
    packed = low(low_back(matmul(normed_one, qkv_full)))
    queries = packed[:, :D].reshape(ROW_LEN, HEADS, HD)
    keys = packed[:, D:2 * D].reshape(ROW_LEN, HEADS, HD)
    values = packed[:, 2 * D:].reshape(ROW_LEN, HEADS, HD)
    attended = low(low_back(self_attention(queries, keys, values, segment_row)))
    after_self = inputs + low_back(matmul(attended, out_full))
    normed_two = low(layer_norm(after_self, gain_two, shift_two))
    cross_queries = low(low_back(matmul(normed_two, query_full))).reshape(ROW_LEN, HEADS, HD)
    context = low(low_back(matmul(text_row.reshape(SEGS * TXT, TD), project_full) + bias_full))
    keyvalue = low(low_back(matmul(context, keyvalue_full)))
    cross_keys = keyvalue[:, :D].reshape(SEGS * TXT, HEADS, HD)
    cross_values = keyvalue[:, D:].reshape(SEGS * TXT, HEADS, HD)
    mixed = low(low_back(cross_attention(cross_queries, cross_keys, cross_values, segment_row, length_row)))
    after_cross = after_self + low_back(matmul(mixed, crossout_full))
    normed_three = low(layer_norm(after_cross, gain_three, shift_three))
    hidden_pre = low_back(matmul(normed_three, feedin_full))
    hidden_low = low(jax.nn.gelu(hidden_pre, approximate=False))
    return after_cross + low_back(matmul(hidden_low, feedout_full))

def reference(frames, segments, text_states, text_lengths, cotangent, self_norm_gain, self_norm_bias, self_qkv, self_output, cross_norm_gain, cross_norm_bias, cross_query, text_project, text_bias, cross_keyvalue, cross_output, feed_norm_gain, feed_norm_bias, feed_in, feed_out):
    params = tuple((weight.astype(jnp.float32) for weight in (self_norm_gain, self_norm_bias, self_qkv, self_output, cross_norm_gain, cross_norm_bias, cross_query, text_project, text_bias, cross_keyvalue, cross_output, feed_norm_gain, feed_norm_bias, feed_in, feed_out)))

    def one_row(totals, row_data):
        inputs, segment_row, text_row, length_row, upstream = row_data

        def forward(input_values, text_values, weights):
            return row_forward(input_values, segment_row, text_values, length_row, weights)
        result, pull = jax.vjp(forward, inputs.astype(jnp.float32), text_row.astype(jnp.float32), params)
        input_grad, text_part, weight_grads = pull(upstream.astype(jnp.float32))
        totals = jax.tree.map(lambda left, right: left + right, totals, weight_grads)
        return (totals, (result.astype(jnp.bfloat16), input_grad.astype(jnp.bfloat16), text_part))
    zeros = tuple((jnp.zeros(weight.shape, jnp.float32) for weight in params))
    totals, (block_out, frames_grad, text_grad) = lax.scan(one_row, zeros, (frames, segments, text_states, text_lengths, cotangent))
    return (block_out, frames_grad, text_grad, totals[0], totals[1], totals[2], totals[3], totals[4], totals[5], totals[6], totals[7], totals[8], totals[9], totals[10], totals[11], totals[12], totals[13], totals[14])
```

```python
import functools

import jax
import jax.numpy as jnp
from jax import lax
from jax.experimental import pallas as pl
from jax.experimental.pallas import tpu as pltpu
from jax.sharding import PartitionSpec as P

HEADS = 16
HD = 64
PAIR = 2 * HD
epsilon = 1e-05
f32 = jnp.float32
bf16 = jnp.bfloat16
HIDE = 2.0 ** 50
MEG = 1024 * 1024


def dot_nn(a, b):
    return lax.dot_general(a, b, (((1,), (0,)), ((), ())), preferred_element_type=f32)


def dot_nt(a, b):
    return lax.dot_general(a, b, (((1,), (1,)), ((), ())), preferred_element_type=f32)


def dot_tn(a, b):
    return lax.dot_general(a, b, (((0,), (0,)), ((), ())), preferred_element_type=f32)


def norm_parts(x):
    mu = jnp.mean(x, axis=-1, keepdims=True)
    xc = x - mu
    rstd = lax.rsqrt(jnp.mean(xc * xc, axis=-1, keepdims=True) + epsilon)
    return xc * rstd, rstd


def norm_pull(n, rstd, gain, dy):
    dn = dy * gain
    dx = rstd * (
        dn - jnp.mean(dn, axis=-1, keepdims=True) - n * jnp.mean(dn * n, axis=-1, keepdims=True)
    )
    return dx


def params(mb, **kw):
    return pltpu.CompilerParams(vmem_limit_bytes=mb * MEG, **kw)


def attn_fwd_kernel(bq, x_ref, g_ref, b_ref, wq_ref, wk_ref, wv_ref, aq_ref, ak_ref,
                    a1_ref, q_ref, k_ref, v_ref, o_ref, lse_ref, kx, vx):
    h = pl.program_id(0)
    n_tok = x_ref.shape[0]
    blocks = n_tok // bq

    @pl.when(h == 0)
    def _():
        gain = g_ref[...].astype(f32)
        bias = b_ref[...].astype(f32)

        @pl.loop(0, blocks)
        def _(i):
            rows = pl.ds(i * bq, bq)
            n, _ = norm_parts(x_ref[rows, :].astype(f32))
            a1_ref[rows, :] = (n * gain + bias).astype(bf16)

        vx[:, PAIR:] = jnp.ones((n_tok, PAIR), bf16)
        kx[:, PAIR:] = ak_ref[...]
        lse_ref[...] = jnp.zeros_like(lse_ref)

    a1 = a1_ref[...]
    q_ref[...] = dot_nn(a1, wq_ref[...]).astype(bf16)
    k = dot_nn(a1, wk_ref[...]).astype(bf16)
    v = dot_nn(a1, wv_ref[...]).astype(bf16)
    k_ref[...] = k
    v_ref[...] = v
    kx[:, :PAIR] = k
    vx[:, :PAIR] = v
    lane = lax.broadcasted_iota(jnp.int32, (bq, PAIR), 1)
    causal = lax.broadcasted_iota(jnp.int32, (bq, bq), 0) >= lax.broadcasted_iota(
        jnp.int32, (bq, bq), 1
    )
    for i in range(blocks):
        rows = slice(i * bq, (i + 1) * bq)
        n = (i + 1) * bq
        q = q_ref[rows, :] * bf16(HD ** -0.5)
        stat = lse_ref[rows, :]
        outs = []
        for half in range(2):
            mine = (lane < HD) if half == 0 else (lane >= HD)
            qx = jnp.concatenate([jnp.where(mine, q, bf16(0)), aq_ref[rows, :]], axis=1)
            s = dot_nt(qx, kx[:n, :])
            last = jnp.where(causal, s[:, n - bq:], -HIDE * HIDE)
            top = jnp.max(last, axis=1, keepdims=True)
            if i:
                top = jnp.maximum(top, jnp.max(s[:, : n - bq], axis=1, keepdims=True))
                p = jnp.concatenate(
                    [jnp.exp(s[:, : n - bq] - top).astype(bf16), jnp.exp(last - top).astype(bf16)],
                    axis=1,
                )
            else:
                p = jnp.exp(last - top).astype(bf16)
            o = dot_nn(p, vx[:n, :])
            total = o[:, PAIR:]
            outs.append(o[:, :PAIR] / total)
            stat = jnp.where(lane == 2 * h + half, top + jnp.log(total), stat)
        o_ref[rows, :] = jnp.where(lane < HD, outs[0], outs[1]).astype(bf16)
        lse_ref[rows, :] = stat


def attn_fwd(x, gain, bias, w_qkv, aug_q, aug_k, bq=256):
    n_tok, width = x.shape
    pairs = width // PAIR
    whole = lambda shape: pl.BlockSpec(shape, lambda h: (0, 0))
    col = lambda off: pl.BlockSpec((width, PAIR), lambda h, off=off: (0, off * pairs + h))
    out_col = pl.BlockSpec((n_tok, PAIR), lambda h: (0, h))
    tall = jax.ShapeDtypeStruct((n_tok, width), bf16)
    return pl.pallas_call(
        functools.partial(attn_fwd_kernel, bq),
        grid=(pairs,),
        in_specs=[whole((n_tok, width)), whole((1, width)), whole((1, width)), col(0), col(1), col(2),
                  whole((n_tok, PAIR)), whole((n_tok, PAIR))],
        out_specs=[whole((n_tok, width)), out_col, out_col, out_col, out_col, whole((n_tok, PAIR))],
        out_shape=[tall, tall, tall, tall, tall, jax.ShapeDtypeStruct((n_tok, PAIR), f32)],
        scratch_shapes=[pltpu.VMEM((n_tok, 2 * PAIR), bf16), pltpu.VMEM((n_tok, 2 * PAIR), bf16)],
        compiler_params=params(56),
        name="self_attention_fwd",
    )(x, gain, bias, w_qkv, w_qkv, w_qkv, aug_q, aug_k)


def cross_fwd_kernel(x_ref, o_ref, wo_ref, g2_ref, b2_ref, wq_ref, kc_ref, vc_ref, aq_ref, ac_ref,
                     wc_ref, g3_ref, b3_ref,
                     x1_ref, a2_ref, qc_ref, oc_ref, x2_ref, a3_ref):
    rows, width = x_ref.shape
    slots = kc_ref.shape[0]
    x1 = x_ref[...].astype(f32) + dot_nn(o_ref[...], wo_ref[...])
    x1_ref[...] = x1
    n, _ = norm_parts(x1)
    a2 = (n * g2_ref[...].astype(f32) + b2_ref[...].astype(f32)).astype(bf16)
    a2_ref[...] = a2
    qc_ref[...] = dot_nn(a2, wq_ref[...]).astype(bf16)
    lane = lax.broadcasted_iota(jnp.int32, (rows, PAIR), 1)
    ones = jnp.ones((slots, PAIR), bf16)
    for h in range(width // PAIR):
        cols = slice(h * PAIR, (h + 1) * PAIR)
        q = qc_ref[:, cols] * bf16(HD ** -0.5)
        kx = jnp.concatenate([kc_ref[:, cols], ac_ref[...]], axis=1)
        vx = jnp.concatenate([vc_ref[:, cols], ones], axis=1)
        outs = []
        for half in range(2):
            mine = (lane < HD) if half == 0 else (lane >= HD)
            qx = jnp.concatenate([jnp.where(mine, q, bf16(0)), aq_ref[...]], axis=1)
            s = dot_nt(qx, kx)
            p = jnp.exp(s - jnp.max(s, axis=1, keepdims=True)).astype(bf16)
            o = dot_nn(p, vx)
            outs.append(o[:, :PAIR] / o[:, PAIR:])
        oc_ref[:, cols] = jnp.where(lane < HD, outs[0], outs[1]).astype(bf16)
    x2 = x1 + dot_nn(oc_ref[...], wc_ref[...])
    x2_ref[...] = x2
    n, _ = norm_parts(x2)
    a3_ref[...] = (n * g3_ref[...].astype(f32) + b3_ref[...].astype(f32)).astype(bf16)


def cross_fwd(x, o, wo, g2, b2, wq, kvc, aug_q, aug_c, wc, g3, b3, rows=512):
    n_tok, width = x.shape
    slots = kvc.shape[0]
    tall = pl.BlockSpec((rows, width), lambda i: (i, 0))
    whole = lambda shape, j=0: pl.BlockSpec(shape, lambda i, j=j: (0, j))
    vec = whole((1, width))
    sq = whole((width, width))
    o16 = jax.ShapeDtypeStruct((n_tok, width), bf16)
    o32 = jax.ShapeDtypeStruct((n_tok, width), f32)
    return pl.pallas_call(
        cross_fwd_kernel,
        grid=(n_tok // rows,),
        in_specs=[tall, tall, sq, vec, vec, sq, whole((slots, width)), whole((slots, width), 1),
                  pl.BlockSpec((rows, PAIR), lambda i: (i, 0)), whole((slots, PAIR)), sq, vec, vec],
        out_specs=[tall] * 6,
        out_shape=[o32, o16, o16, o16, o32, o16],
        compiler_params=params(56),
        name="cross_attention_fwd",
    )(x, o, wo, g2, b2, wq, kvc, kvc, aug_q, aug_c, wc, g3, b3)


def gelu_and_slope(u):
    a = jnp.abs(u)
    t = 1.0 / (1.0 + (0.3275911 * 0.7071067811865476) * a)
    e = jnp.exp(-0.5 * (u * u))
    poly = t * (0.254829592 + t * (-0.284496736 + t * (1.421413741 + t * (-1.453152027 + t * 1.061405429))))
    tail = (0.5 * poly) * e
    phi = jnp.where(u >= 0, 1.0 - tail, tail)
    return u * phi, phi + u * (e * 0.3989422804014327)


def feed_kernel(rows, a3_ref, g_ref, x2_ref, gain_ref, bias_ref, wi_ref, wo_ref,
                out_ref, dx2_ref, gi_ref, go_ref, dgain_ref, dbias_ref, acc, da3, a3t, gl, du):
    c = pl.program_id(0)
    n_tok, width = a3_ref.shape
    blocks = n_tok // rows

    @pl.when(c == 0)
    def _():
        a3t[...] = a3_ref[...].T

    @pl.loop(0, blocks)
    def _(i):
        r = pl.ds(i * rows, rows)
        up = g_ref[r, :]
        u = dot_nn(a3_ref[r, :], wi_ref[...])
        act, slope = gelu_and_slope(u)
        act = act.astype(bf16)
        gl[r, :] = act
        y = dot_nn(act, wo_ref[...])
        d = (dot_nt(up, wo_ref[...]) * slope).astype(bf16)
        du[r, :] = d
        da = dot_nt(d, wi_ref[...])

        @pl.when(c == 0)
        def _():
            acc[r, :] = y
            da3[r, :] = da

        @pl.when(c > 0)
        def _():
            acc[r, :] += y
            da3[r, :] += da

    gi_ref[...] = dot_nn(a3t[...], du[...]).astype(bf16)
    go_ref[...] = dot_tn(gl[...], g_ref[...]).astype(bf16)

    @pl.when(c == pl.num_programs(0) - 1)
    def _():
        gain = gain_ref[...].astype(f32)
        dgain_ref[...] = jnp.zeros_like(dgain_ref)
        dbias_ref[...] = jnp.zeros_like(dbias_ref)

        @pl.loop(0, blocks * 2)
        def _(i):
            r = pl.ds(i * (rows // 2), rows // 2)
            x2 = x2_ref[r, :]
            out_ref[r, :] = (x2 + acc[r, :]).astype(bf16)
            n, rstd = norm_parts(x2)
            dy = da3[r, :]
            dx2_ref[r, :] = g_ref[r, :].astype(f32) + norm_pull(n, rstd, gain, dy)
            dgain_ref[...] += jnp.sum(dy * n, axis=0, keepdims=True)
            dbias_ref[...] += jnp.sum(dy, axis=0, keepdims=True)


def feed(a3, g, x2, gain, bias, w_in, w_out, rows=512, cols=512):
    n_tok, width = a3.shape
    hidden = w_in.shape[1]
    whole = lambda shape: pl.BlockSpec(shape, lambda c: (0, 0), pipeline_mode=pl.Buffered(1))
    out_whole = lambda shape: pl.BlockSpec(shape, lambda c: (0, 0))
    wi = pl.BlockSpec((width, cols), lambda c: (0, c))
    wo = pl.BlockSpec((cols, width), lambda c: (c, 0))
    S = jax.ShapeDtypeStruct
    return pl.pallas_call(
        functools.partial(feed_kernel, rows),
        grid=(hidden // cols,),
        in_specs=[whole((n_tok, width)), whole((n_tok, width)), whole((n_tok, width)),
                  whole((1, width)), whole((1, width)), wi, wo],
        out_specs=[whole((n_tok, width)), whole((n_tok, width)), wi, wo,
                   out_whole((1, width)), out_whole((1, width))],
        out_shape=[S((n_tok, width), bf16), S((n_tok, width), f32), S((width, hidden), bf16),
                   S((hidden, width), bf16), S((1, width), f32), S((1, width), f32)],
        scratch_shapes=[pltpu.VMEM((n_tok, width), f32), pltpu.VMEM((n_tok, width), f32),
                        pltpu.VMEM((width, n_tok), bf16), pltpu.VMEM((n_tok, cols), bf16),
                        pltpu.VMEM((n_tok, cols), bf16)],
        compiler_params=params(60),
        name="feed_forward_both",
    )(a3, g, x2, gain, bias, w_in, w_out)


def cross_bwd_kernel(dx2_ref, oc_ref, a2_ref, qc_ref, x1_ref, o_ref, aq_ref, ac_ref, kc_ref, vc_ref,
                     wc_ref, wq_ref, wo_ref, g2_ref, e_ref,
                     gc_ref, gq_ref, go_ref, dkv_ref, dx1_ref, do_ref, delta_ref, dgain_ref, dbias_ref,
                     acc_c, acc_q, acc_o, acc_kv, doc, dqc):
    i = pl.program_id(0)
    rows, width = dx2_ref.shape
    slots = kc_ref.shape[0]

    @pl.when(i == 0)
    def _():
        acc_c[...] = jnp.zeros_like(acc_c)
        acc_q[...] = jnp.zeros_like(acc_q)
        acc_o[...] = jnp.zeros_like(acc_o)
        acc_kv[...] = jnp.zeros_like(acc_kv)
        dgain_ref[...] = jnp.zeros_like(dgain_ref)
        dbias_ref[...] = jnp.zeros_like(dbias_ref)

    g2 = dx2_ref[...].astype(bf16)
    acc_c[...] += dot_tn(oc_ref[...], g2)
    doc[...] = dot_nt(g2, wc_ref[...]).astype(bf16)
    lane = lax.broadcasted_iota(jnp.int32, (rows, PAIR), 1)
    slot_lane = lax.broadcasted_iota(jnp.int32, (slots, PAIR), 1)
    ones = jnp.ones((slots, PAIR), bf16)
    for h in range(width // PAIR):
        cols = slice(h * PAIR, (h + 1) * PAIR)
        q = qc_ref[:, cols] * bf16(HD ** -0.5)
        up = doc[:, cols]
        k = kc_ref[:, cols]
        v = vc_ref[:, cols]
        kx = jnp.concatenate([k, ac_ref[...]], axis=1)
        dqs, dks, dvs = [], [], []
        for half in range(2):
            mine = (lane < HD) if half == 0 else (lane >= HD)
            qx = jnp.concatenate([jnp.where(mine, q, bf16(0)), aq_ref[...]], axis=1)
            s = dot_nt(qx, kx)
            w = jnp.exp(s - jnp.max(s, axis=1, keepdims=True))
            p = w / jnp.sum(w, axis=1, keepdims=True)
            dp = dot_nt(jnp.where(mine, up, bf16(0)), v)
            ds = (p * (dp - jnp.sum(dp * p, axis=1, keepdims=True))).astype(bf16)
            dqs.append(dot_nn(ds, k))
            dks.append(dot_tn(ds, q))
            dvs.append(dot_tn(p.astype(bf16), up))
        dqc[:, cols] = (jnp.where(lane < HD, dqs[0], dqs[1]) * (HD ** -0.5)).astype(bf16)
        acc_kv[:, cols] += jnp.where(slot_lane < HD, dks[0], dks[1])
        v_cols = slice(width + h * PAIR, width + (h + 1) * PAIR)
        acc_kv[:, v_cols] += jnp.where(slot_lane < HD, dvs[0], dvs[1])
    dq = dqc[...]
    acc_q[...] += dot_tn(a2_ref[...], dq)
    dy = dot_nt(dq, wq_ref[...])
    n, rstd = norm_parts(x1_ref[...])
    dgain_ref[...] += jnp.sum(dy * n, axis=0, keepdims=True)
    dbias_ref[...] += jnp.sum(dy, axis=0, keepdims=True)
    dx1 = dx2_ref[...] + norm_pull(n, rstd, g2_ref[...].astype(f32), dy)
    dx1_ref[...] = dx1
    g1 = dx1.astype(bf16)
    o = o_ref[...]
    acc_o[...] += dot_tn(o, g1)
    do = dot_nt(g1, wo_ref[...]).astype(bf16)
    do_ref[...] = do
    prod = do.astype(f32) * o.astype(f32)
    hi = prod.astype(bf16)
    lo = (prod - hi.astype(f32)).astype(bf16)
    delta_ref[...] = dot_nn(hi, e_ref[...]) + dot_nn(lo, e_ref[...])

    @pl.when(i == pl.num_programs(0) - 1)
    def _():
        gc_ref[...] = acc_c[...].astype(bf16)
        gq_ref[...] = acc_q[...].astype(bf16)
        go_ref[...] = acc_o[...].astype(bf16)
        dkv_ref[...] = acc_kv[...].astype(bf16)


def cross_bwd(dx2, oc, a2, qc, x1, o, aug_q, aug_c, kvc, wc, wq, wo, g2, head_sum, rows=256):
    n_tok, width = dx2.shape
    slots = kvc.shape[0]
    tall = pl.BlockSpec((rows, width), lambda i: (i, 0))
    thin = pl.BlockSpec((rows, PAIR), lambda i: (i, 0))
    whole = lambda shape, j=0: pl.BlockSpec(shape, lambda i, j=j: (0, j), pipeline_mode=pl.Buffered(1))
    once = lambda shape: pl.BlockSpec(shape, lambda i: (0, 0), pipeline_mode=pl.Buffered(1))
    out_vec = pl.BlockSpec((1, width), lambda i: (0, 0))
    sq = whole((width, width))
    S = jax.ShapeDtypeStruct
    return pl.pallas_call(
        cross_bwd_kernel,
        grid=(n_tok // rows,),
        in_specs=[tall, tall, tall, tall, tall, tall, thin, whole((slots, PAIR)),
                  whole((slots, width)), whole((slots, width), 1), sq, sq, sq, whole((1, width)),
                  whole((width, PAIR))],
        out_specs=[once((width, width))] * 3 + [once((slots, 2 * width)), tall, tall, thin, out_vec, out_vec],
        out_shape=[S((width, width), bf16)] * 3 + [
            S((slots, 2 * width), bf16), S((n_tok, width), f32), S((n_tok, width), bf16),
            S((n_tok, PAIR), f32), S((1, width), f32), S((1, width), f32)],
        scratch_shapes=[pltpu.VMEM((width, width), f32)] * 3 + [
            pltpu.VMEM((slots, 2 * width), f32), pltpu.VMEM((rows, width), bf16),
            pltpu.VMEM((rows, width), bf16)],
        compiler_params=params(60),
        name="cross_attention_bwd",
    )(dx2, oc, a2, qc, x1, o, aug_q, aug_c, kvc, kvc, wc, wq, wo, g2, head_sum)


def three_parts(v):
    hi = v.astype(bf16)
    rest = v - hi.astype(f32)
    mid = rest.astype(bf16)
    return hi, mid, (rest - mid.astype(f32)).astype(bf16)


def attn_bwd_kernel(bk, q_ref, k_ref, v_ref, do_ref, lse_ref, delta_ref, aq_ref, ak_ref, a1_ref, x_ref,
                    dx1_ref, gain_ref, wq_ref, wk_ref, wv_ref,
                    gq_ref, gk_ref, gv_ref, dx_ref, dgain_ref, dbias_ref,
                    a1t, da1, qx, dox, dq, dkv):
    h = pl.program_id(0)
    n_tok, width = a1_ref.shape
    blocks = n_tok // bk

    @pl.when(h == 0)
    def _():
        a1t[...] = a1_ref[...].T
        da1[...] = jnp.zeros_like(da1)

    lane = lax.broadcasted_iota(jnp.int32, (n_tok, PAIR), 1)
    lane_k = lax.broadcasted_iota(jnp.int32, (bk, PAIR), 1)
    causal = lax.broadcasted_iota(jnp.int32, (bk, bk), 0) <= lax.broadcasted_iota(
        jnp.int32, (bk, bk), 1
    )
    q = q_ref[...] * bf16(HD ** -0.5)
    up = do_ref[...]
    for half in range(2):
        mine = (lane < HD) if half == 0 else (lane >= HD)
        col = lane == 2 * h + half
        lse = jnp.sum(jnp.where(col, lse_ref[...], 0.0), axis=1, keepdims=True)
        dlt = jnp.sum(jnp.where(col, delta_ref[...], 0.0), axis=1, keepdims=True)
        l_hi, l_mid, l_lo = three_parts(jnp.broadcast_to(-lse, (n_tok, PAIR)))
        d_hi, d_mid, d_lo = three_parts(jnp.broadcast_to(-dlt, (n_tok, PAIR)))
        zero = jnp.zeros((n_tok, PAIR), bf16)

        def place(base, hi, mid, lo):
            return jnp.where(lane == 8, hi, jnp.where(lane == 9, mid, jnp.where(lane == 10, lo, base)))

        qx[:, :PAIR] = jnp.where(mine, q, bf16(0))
        qx[:, PAIR:] = place(aq_ref[...], l_hi, l_mid, l_lo)
        dox[:, :PAIR] = jnp.where(mine, up, bf16(0))
        dox[:, PAIR:] = place(zero, d_hi, d_mid, d_lo)
        unit = ((lane_k >= 8) & (lane_k <= 10)).astype(bf16)
        for j in range(blocks):
            rows = slice(j * bk, (j + 1) * bk)
            rest = slice(j * bk, n_tok)
            k = k_ref[rows, :]
            s = dot_nt(jnp.concatenate([k, ak_ref[rows, :] + unit], axis=1), qx[rest, :])
            head = jnp.where(causal, s[:, :bk], -HIDE * HIDE)
            s = jnp.concatenate([head, s[:, bk:]], axis=1) if j < blocks - 1 else head
            p = jnp.exp(s)
            dp = dot_nt(jnp.concatenate([v_ref[rows, :], unit], axis=1), dox[rest, :])
            ds = (p * dp).astype(bf16)
            dv = dot_nn(p.astype(bf16), dox[rest, :PAIR])
            dk = dot_nn(ds, qx[rest, :PAIR])
            if half == 0:
                dkv[rows, :PAIR] = dk
                dkv[rows, PAIR:] = dv
            else:
                dkv[rows, :PAIR] += dk
                dkv[rows, PAIR:] += dv
            part = dot_tn(ds, k)
            keep = (lane[rest, :] < HD) if half == 0 else (lane[rest, :] >= HD)
            part = jnp.where(keep, part, 0.0)
            if half == 0 and j == 0:
                dq[...] = part
            else:
                dq[rest, :] += part
    dq16 = (dq[...] * (HD ** -0.5)).astype(bf16)
    dk16 = dkv[:, :PAIR].astype(bf16)
    dv16 = dkv[:, PAIR:].astype(bf16)
    gq_ref[...] = dot_nn(a1t[...], dq16).astype(bf16)
    gk_ref[...] = dot_nn(a1t[...], dk16).astype(bf16)
    gv_ref[...] = dot_nn(a1t[...], dv16).astype(bf16)
    d3 = jnp.concatenate([dq16, dk16, dv16], axis=1)
    w3 = jnp.concatenate([wq_ref[...], wk_ref[...], wv_ref[...]], axis=1)
    da1[...] += dot_nt(d3, w3)

    @pl.when(h == pl.num_programs(0) - 1)
    def _():
        gain = gain_ref[...].astype(f32)
        dgain_ref[...] = jnp.zeros_like(dgain_ref)
        dbias_ref[...] = jnp.zeros_like(dbias_ref)

        @pl.loop(0, blocks)
        def _(i):
            r = pl.ds(i * bk, bk)
            n, rstd = norm_parts(x_ref[r, :].astype(f32))
            dy = da1[r, :]
            dx_ref[r, :] = (dx1_ref[r, :] + norm_pull(n, rstd, gain, dy)).astype(bf16)
            dgain_ref[...] += jnp.sum(dy * n, axis=0, keepdims=True)
            dbias_ref[...] += jnp.sum(dy, axis=0, keepdims=True)


def attn_bwd(q, k, v, do, lse, delta, aug_q, aug_k, a1, x, dx1, gain, w_qkv, bk=256):
    n_tok, width = x.shape
    pairs = width // PAIR
    whole = lambda shape: pl.BlockSpec(shape, lambda h: (0, 0), pipeline_mode=pl.Buffered(1))
    vec = pl.BlockSpec((1, width), lambda h: (0, 0))
    tall = pl.BlockSpec((n_tok, PAIR), lambda h: (0, h))
    wcol = lambda off: pl.BlockSpec((width, PAIR), lambda h, off=off: (0, off * pairs + h))
    S = jax.ShapeDtypeStruct
    return pl.pallas_call(
        functools.partial(attn_bwd_kernel, bk),
        grid=(pairs,),
        in_specs=[tall, tall, tall, tall, whole((n_tok, PAIR)), whole((n_tok, PAIR)),
                  whole((n_tok, PAIR)), whole((n_tok, PAIR)), whole((n_tok, width)),
                  whole((n_tok, width)), whole((n_tok, width)), vec, wcol(0), wcol(1), wcol(2)],
        out_specs=[wcol(0), wcol(0), wcol(0), whole((n_tok, width)), vec, vec],
        out_shape=[S((width, width), bf16)] * 3 + [S((n_tok, width), bf16), S((1, width), f32), S((1, width), f32)],
        scratch_shapes=[pltpu.VMEM((width, n_tok), bf16), pltpu.VMEM((n_tok, width), f32),
                        pltpu.VMEM((n_tok, 2 * PAIR), bf16), pltpu.VMEM((n_tok, 2 * PAIR), bf16),
                        pltpu.VMEM((n_tok, PAIR), f32), pltpu.VMEM((n_tok, 2 * PAIR), f32)],
        compiler_params=params(60),
        name="self_attention_bwd",
    )(q, k, v, do, lse, delta, aug_q, aug_k, a1, x, dx1, gain, w_qkv, w_qkv, w_qkv)


def spread_sum(part, order, steps):
    at = lax.axis_index("dp")
    place = {"z": at // 4, "y": (at // 2) % 2, "c": at % 2, "x": lax.axis_index("seq")}
    names = ["z", "y", "c", "x"]
    for step in order:
        name = step[0]
        axis = names.index(name)
        size = part.shape[axis]
        if name == "x":
            pairs, mesh_axis = [(0, 1), (1, 0)], "seq"
            mine = place["x"]
        else:
            flip = {"y": 2, "c": 1, "zh": 8, "zl": 4}[step]
            pairs, mesh_axis = [(i, i ^ flip) for i in range(16)], "dp"
            mine = {"y": place["y"], "c": place["c"], "zh": place["z"] // 2, "zl": place["z"] % 2}[step]
        half = size // 2
        keep = lax.dynamic_slice_in_dim(part, mine * half, half, axis)
        give = lax.dynamic_slice_in_dim(part, (1 - mine) * half, half, axis)
        got = lax.ppermute(give, mesh_axis, pairs)
        part = (keep.astype(f32) + got.astype(f32)).astype(bf16)
    return part.reshape(part.shape[4:]).astype(f32)


def per_device_rows(
    frames, segments, text_states, text_lengths, cotangent,
    self_norm_gain, self_norm_bias, self_qkv, self_output,
    cross_norm_gain, cross_norm_bias, cross_query, text_project, text_bias,
    cross_keyvalue, cross_output, feed_norm_gain, feed_norm_bias, feed_in, feed_out,
):
    at = lax.axis_index("seq")
    _, half, width = frames.shape
    n_tok = 2 * half
    everywhere = ("dp", "seq")
    flip = [(0, 1), (1, 0)]

    def swap_in(v):
        mine = lax.dynamic_index_in_dim(v, at, 0, keepdims=False)
        got = lax.ppermute(lax.dynamic_index_in_dim(v, 1 - at, 0, keepdims=False), "seq", flip)
        return jnp.where(at == 0, jnp.concatenate([mine, got]), jnp.concatenate([got, mine]))

    def swap_out(v):
        mine = lax.dynamic_slice_in_dim(v, at * half, half, 0)
        got = lax.ppermute(lax.dynamic_slice_in_dim(v, (1 - at) * half, half, 0), "seq", flip)
        return jnp.where(at == 0, jnp.stack([mine, got]), jnp.stack([got, mine]))

    gather = lambda v: lax.all_gather(v, everywhere, axis=0, tiled=True)

    vectors = jnp.stack([self_norm_gain, self_norm_bias, cross_norm_gain, cross_norm_bias,
                         text_bias, feed_norm_gain, feed_norm_bias])
    vectors = lax.all_gather(vectors, everywhere, axis=1, tiled=True)
    vec = lambda i: vectors[i][None, :]
    x = swap_in(frames)
    seg = swap_in(segments)
    w_qkv = gather(self_qkv)
    w_o = gather(self_output)
    w_q = gather(cross_query)
    w_p = gather(text_project)
    w_kv = gather(cross_keyvalue)
    w_c = gather(cross_output)
    w_i = gather(feed_in)
    w_f = gather(feed_out)
    up = swap_in(cotangent)

    clips, txt, text_width = text_states.shape[1:]
    slots = clips * txt
    lane = jnp.arange(PAIR, dtype=jnp.int32)[None, :]
    aug_q = jnp.where(lane == seg[:, None], -HIDE, 0.0).astype(bf16)
    aug_k = jnp.where((lane < 4) & (lane != seg[:, None]), HIDE, 0.0).astype(bf16)
    lengths = lax.dynamic_index_in_dim(text_lengths, at, 0, keepdims=False)
    slot = jnp.arange(slots, dtype=jnp.int32)
    live = (slot % txt) < jnp.repeat(lengths, txt)
    aug_c = jnp.where((lane < 4) & ~((lane == (slot // txt)[:, None]) & live[:, None]), HIDE, 0.0).astype(bf16)

    a1, q, k, v, o, lse = attn_fwd(x, vec(0), vec(1), w_qkv, aug_q, aug_k)

    text = lax.dynamic_index_in_dim(text_states, at, 0, keepdims=False).reshape(slots, text_width)
    context = (dot_nn(text, w_p) + vec(4).astype(f32)).astype(bf16)
    kvc = dot_nn(context, w_kv).astype(bf16)
    x1, a2, qc, oc, x2, a3 = cross_fwd(x, o, w_o, vec(2), vec(3), w_q, kvc, aug_q, aug_c, w_c, vec(5), vec(6))

    block_out, dx2, g_i, g_f, dgain3, dbias3 = feed(a3, up, x2, vec(5), vec(6), w_i, w_f)

    head_sum = (jnp.arange(width, dtype=jnp.int32)[:, None] // HD == lane).astype(bf16)
    g_c, g_q, g_o, dkv, dx1, do, delta, dgain2, dbias2 = cross_bwd(
        dx2, oc, a2, qc, x1, o, aug_q, aug_c, kvc, w_c, w_q, w_o, vec(2), head_sum)

    g_kv = dot_tn(context, dkv).astype(bf16)
    dc = dot_nt(dkv, w_kv).astype(bf16)
    g_p = dot_tn(text, dc).astype(bf16)
    dbias_t = jnp.sum(dc.astype(f32), axis=0)
    text_grad = dot_nt(dc, w_p).reshape(clips, txt, text_width)
    th = txt // 2
    t_mine = lax.dynamic_slice_in_dim(text_grad, at * th, th, 1)
    t_got = lax.ppermute(lax.dynamic_slice_in_dim(text_grad, (1 - at) * th, th, 1), "seq", flip)
    text_out = jnp.where(at == 0, jnp.stack([t_mine, t_got]), jnp.stack([t_got, t_mine]))

    g_wq, g_wk, g_wv, dx, dgain1, dbias1 = attn_bwd(
        q, k, v, do, lse, delta, aug_q, aug_k, a1, x, dx1, vec(0), w_qkv)

    def total(g, order):
        rows = g.shape[0] // 32
        return spread_sum(g.reshape((4, 2, 2, 2, rows) + g.shape[1:]), order, None)

    xy = ["c", "x", "y", "zh", "zl"]
    yx = ["c", "y", "x", "zh", "zl"]
    s_i = total(g_i, xy)
    s_f = total(g_f, yx)
    s_c = total(g_c, xy)
    s_q = total(g_q, yx)
    s_o = total(g_o, xy)
    s_kv = total(g_kv, yx)
    s_p = total(g_p, xy)
    s_wq = total(g_wq, xy)
    s_wk = total(g_wk, yx)
    s_wv = total(g_wv, xy)
    s_qkv = jnp.concatenate([s_wq, s_wk, s_wv], axis=1)
    vecs = jnp.concatenate([dgain1, dbias1, dgain2, dbias2, dbias_t[None, :], dgain3, dbias3])
    vecs = lax.psum_scatter(vecs, everywhere, scatter_dimension=1, tiled=True)
    return (
        swap_out(block_out), swap_out(dx), text_out, vecs[0], vecs[1], s_qkv, s_o, vecs[2], vecs[3],
        s_q, s_p, vecs[4], s_kv, s_c, vecs[5], vecs[6], s_i, s_f,
    )


big_negative = -1e30


def layer_norm(values, gain, shift):
    centre = jnp.mean(values, axis=-1, keepdims=True)
    centred = values - centre
    spread = jnp.mean(centred * centred, axis=-1, keepdims=True)
    return centred * lax.rsqrt(spread + epsilon) * gain + shift


def norm_back(values, gain, shift, upstream):
    _, pull = jax.vjp(layer_norm, values, gain, shift)
    return pull(upstream)


def gelu_exact(values):
    return jax.nn.gelu(values, approximate=False)


def matmul(left, right):
    return jnp.dot(left, right, preferred_element_type=jnp.float32)


def left_tmul(left, right):
    return lax.dot_general(
        left, right, (((0,), (0,)), ((), ())), preferred_element_type=jnp.float32
    )


def right_tmul(left, right):
    return lax.dot_general(
        left, right, (((1,), (1,)), ((), ())), preferred_element_type=jnp.float32
    )


def per_device(
    frames,
    segments,
    text_states,
    text_lengths,
    cotangent,
    self_norm_gain,
    self_norm_bias,
    self_qkv,
    self_output,
    cross_norm_gain,
    cross_norm_bias,
    cross_query,
    text_project,
    text_bias,
    cross_keyvalue,
    cross_output,
    feed_norm_gain,
    feed_norm_bias,
    feed_in,
    feed_out,
):
    shards = (
        self_norm_gain,
        self_norm_bias,
        self_qkv,
        self_output,
        cross_norm_gain,
        cross_norm_bias,
        cross_query,
        text_project,
        text_bias,
        cross_keyvalue,
        cross_output,
        feed_norm_gain,
        feed_norm_bias,
        feed_in,
        feed_out,
    )
    gathered = (
        lax.all_gather(shards[0], ("dp", "seq"), axis=0, tiled=True),
        lax.all_gather(shards[1], ("dp", "seq"), axis=0, tiled=True),
        lax.all_gather(shards[2], ("dp", "seq"), axis=0, tiled=True),
        lax.all_gather(shards[3], ("dp", "seq"), axis=0, tiled=True),
        lax.all_gather(shards[4], ("dp", "seq"), axis=0, tiled=True),
        lax.all_gather(shards[5], ("dp", "seq"), axis=0, tiled=True),
        lax.all_gather(shards[6], ("dp", "seq"), axis=0, tiled=True),
        lax.all_gather(shards[7], ("dp", "seq"), axis=0, tiled=True),
        lax.all_gather(shards[8], ("dp", "seq"), axis=0, tiled=True),
        lax.all_gather(shards[9], ("dp", "seq"), axis=0, tiled=True),
        lax.all_gather(shards[10], ("dp", "seq"), axis=0, tiled=True),
        lax.all_gather(shards[11], ("dp", "seq"), axis=0, tiled=True),
        lax.all_gather(shards[12], ("dp", "seq"), axis=0, tiled=True),
        lax.all_gather(shards[13], ("dp", "seq"), axis=0, tiled=True),
        lax.all_gather(shards[14], ("dp", "seq"), axis=0, tiled=True),
    )
    (
        gain_one,
        shift_one,
        qkv_full,
        out_full,
        gain_two,
        shift_two,
        query_full,
        project_full,
        bias_full,
        keyvalue_full,
        crossout_full,
        gain_three,
        shift_three,
        feedin_full,
        feedout_full,
    ) = gathered
    f32 = jnp.float32
    bf16 = jnp.bfloat16
    row_count, frame_count, width = frames.shape
    token_count = row_count * frame_count
    head_count = HEADS
    head_size = HD
    scale = head_size ** (-0.5)
    seq_index = lax.axis_index("seq")
    query_pos = seq_index * frame_count + jnp.arange(frame_count, dtype=jnp.int32)
    all_segments = lax.all_gather(segments, "seq", axis=1, tiled=True)

    def visible(count):
        key_pos = jnp.arange(count, dtype=jnp.int32)
        causal = key_pos[None, None, :] <= query_pos[None, :, None]
        same_clip = all_segments[:, None, :] == segments[:, :, None]
        return (causal & same_clip)[:, None]

    inputs = frames.astype(f32).reshape(token_count, width)
    normed_one = layer_norm(inputs, gain_one.astype(f32), shift_one.astype(f32)).astype(bf16)
    packed = matmul(normed_one, qkv_full).astype(bf16)
    queries = packed[:, :width].reshape(row_count, frame_count, head_count, head_size)
    keys_own = packed[:, width : 2 * width].reshape(row_count, frame_count, width)
    values_own = packed[:, 2 * width :].reshape(row_count, frame_count, width)
    key_heads_own = keys_own.reshape(row_count, frame_count, head_count, head_size)
    value_heads_own = values_own.reshape(row_count, frame_count, head_count, head_size)
    running = jnp.full((row_count, head_count, frame_count), big_negative, f32)
    key_piece = lax.all_gather(keys_own, "seq", axis=1, tiled=True)
    value_piece = lax.all_gather(values_own, "seq", axis=1, tiled=True)
    count = key_piece.shape[1]
    key_heads = key_piece.reshape(row_count, count, head_count, head_size)
    value_heads = value_piece.reshape(row_count, count, head_count, head_size)
    scores = jnp.einsum("rqhd,rkhd->rhqk", queries, key_heads, preferred_element_type=f32) * scale
    allowed = visible(count)
    masked = jnp.where(allowed, scores, big_negative)
    fresh = jnp.maximum(running, jnp.max(masked, axis=-1))
    weights = jnp.where(allowed, jnp.exp(masked - fresh[..., None]), 0.0)
    total = jnp.sum(weights, axis=-1)
    accum = jnp.einsum(
        "rhqk,rkhd->rhqd", weights.astype(bf16), value_heads, preferred_element_type=f32
    )
    running, total, accum = (fresh, total, accum)
    attended = accum / total[..., None]
    log_total = running + jnp.log(total)
    attended_low = attended.transpose(0, 2, 1, 3).reshape(token_count, width).astype(bf16)
    after_self = inputs + matmul(attended_low, out_full)
    normed_two = layer_norm(after_self, gain_two.astype(f32), shift_two.astype(f32)).astype(bf16)
    cross_queries = (
        matmul(normed_two, query_full)
        .astype(bf16)
        .reshape(row_count, frame_count, head_count, head_size)
    )
    clip_count, text_count, text_width = text_states.shape[1:]
    slot_total = clip_count * text_count
    text_flat = text_states.reshape(row_count * slot_total, text_width)
    context = (matmul(text_flat, project_full) + bias_full.astype(f32)).astype(bf16)
    keyvalue = matmul(context, keyvalue_full).astype(bf16).reshape(row_count, slot_total, 2 * width)
    cross_keys = keyvalue[..., :width].reshape(row_count, slot_total, head_count, head_size)
    cross_values = keyvalue[..., width:].reshape(row_count, slot_total, head_count, head_size)
    slot_ids = jnp.arange(slot_total, dtype=jnp.int32)
    key_clip = slot_ids // text_count
    key_slot = slot_ids % text_count
    live = key_slot[None, :] < jnp.repeat(text_lengths, text_count, axis=1)
    cross_allowed = ((segments[:, :, None] == key_clip[None, None, :]) & live[:, None, :])[:, None]
    cross_scores = (
        jnp.einsum("rqhd,rkhd->rhqk", cross_queries, cross_keys, preferred_element_type=f32) * scale
    )
    cross_masked = jnp.where(cross_allowed, cross_scores, big_negative)
    cross_top = jnp.max(cross_masked, axis=-1, keepdims=True)
    cross_weights = jnp.where(cross_allowed, jnp.exp(cross_masked - cross_top), 0.0)
    cross_prob = cross_weights / jnp.sum(cross_weights, axis=-1, keepdims=True)
    cross_low = cross_prob.astype(bf16)
    cross_mixed = jnp.einsum("rhqk,rkhd->rqhd", cross_low, cross_values, preferred_element_type=f32)
    cross_mixed_low = cross_mixed.reshape(token_count, width).astype(bf16)
    after_cross = after_self + matmul(cross_mixed_low, crossout_full)
    normed_three = layer_norm(after_cross, gain_three.astype(f32), shift_three.astype(f32)).astype(
        bf16
    )
    hidden_pre = matmul(normed_three, feedin_full)
    hidden_low = gelu_exact(hidden_pre).astype(bf16)
    result = after_cross + matmul(hidden_low, feedout_full)
    block_out = result.astype(bf16).reshape(row_count, frame_count, width)
    regathered = (
        lax.all_gather(shards[0], ("dp", "seq"), axis=0, tiled=True),
        lax.all_gather(shards[1], ("dp", "seq"), axis=0, tiled=True),
        lax.all_gather(shards[2], ("dp", "seq"), axis=0, tiled=True),
        lax.all_gather(shards[3], ("dp", "seq"), axis=0, tiled=True),
        lax.all_gather(shards[4], ("dp", "seq"), axis=0, tiled=True),
        lax.all_gather(shards[5], ("dp", "seq"), axis=0, tiled=True),
        lax.all_gather(shards[6], ("dp", "seq"), axis=0, tiled=True),
        lax.all_gather(shards[7], ("dp", "seq"), axis=0, tiled=True),
        lax.all_gather(shards[8], ("dp", "seq"), axis=0, tiled=True),
        lax.all_gather(shards[9], ("dp", "seq"), axis=0, tiled=True),
        lax.all_gather(shards[10], ("dp", "seq"), axis=0, tiled=True),
        lax.all_gather(shards[11], ("dp", "seq"), axis=0, tiled=True),
        lax.all_gather(shards[12], ("dp", "seq"), axis=0, tiled=True),
        lax.all_gather(shards[13], ("dp", "seq"), axis=0, tiled=True),
        lax.all_gather(shards[14], ("dp", "seq"), axis=0, tiled=True),
    )
    (
        gain_one_b,
        shift_one_b,
        qkv_back,
        out_back,
        gain_two_b,
        shift_two_b,
        query_back,
        project_back,
        bias_back,
        keyvalue_back,
        crossout_back,
        gain_three_b,
        shift_three_b,
        feedin_back,
        feedout_back,
    ) = regathered
    upstream = cotangent.astype(f32).reshape(token_count, width)
    upstream_low = cotangent.reshape(token_count, width)
    feedout_grad = left_tmul(hidden_low, upstream_low)
    hidden_grad = right_tmul(upstream_low, feedout_back)
    _, gelu_pull = jax.vjp(gelu_exact, hidden_pre)
    (pre_grad,) = gelu_pull(hidden_grad)
    pre_grad_low = pre_grad.astype(bf16)
    feedin_grad = left_tmul(normed_three, pre_grad_low)
    normed_three_grad = right_tmul(pre_grad_low, feedin_back)
    cross_res_grad, gain_three_grad, shift_three_grad = norm_back(
        after_cross, gain_three_b.astype(f32), shift_three_b.astype(f32), normed_three_grad
    )
    after_cross_grad = upstream + cross_res_grad
    cross_branch_low = after_cross_grad.astype(bf16)
    crossout_grad = left_tmul(cross_mixed_low, cross_branch_low)
    mixed_grad = (
        right_tmul(cross_branch_low, crossout_back)
        .astype(bf16)
        .reshape(row_count, frame_count, head_count, head_size)
    )
    prob_grad = jnp.einsum("rqhd,rkhd->rhqk", mixed_grad, cross_values, preferred_element_type=f32)
    cross_values_grad = jnp.einsum(
        "rhqk,rqhd->rkhd", cross_low, mixed_grad, preferred_element_type=f32
    )
    cross_score_low = (
        cross_prob * (prob_grad - jnp.sum(prob_grad * cross_prob, axis=-1, keepdims=True))
    ).astype(bf16)
    cross_queries_grad = (
        (
            jnp.einsum("rhqk,rkhd->rqhd", cross_score_low, cross_keys, preferred_element_type=f32)
            * scale
        )
        .astype(bf16)
        .reshape(token_count, width)
    )
    cross_keys_grad = (
        jnp.einsum("rhqk,rqhd->rkhd", cross_score_low, cross_queries, preferred_element_type=f32)
        * scale
    )
    keyvalue_part = jnp.concatenate(
        [
            cross_keys_grad.reshape(row_count, clip_count, text_count, width),
            cross_values_grad.reshape(row_count, clip_count, text_count, width),
        ],
        axis=3,
    )
    keyvalue_grad = (
        lax.psum_scatter(keyvalue_part.astype(jnp.bfloat16), "seq", scatter_dimension=2, tiled=True)
        .astype(jnp.float32)
        .astype(bf16)
    )
    slot_count = keyvalue_grad.shape[2]
    context_slice = lax.dynamic_slice_in_dim(
        context.reshape(row_count, clip_count, text_count, width),
        seq_index * slot_count,
        slot_count,
        2,
    ).reshape(row_count * clip_count * slot_count, width)
    text_slice = lax.dynamic_slice_in_dim(
        text_states, seq_index * slot_count, slot_count, 2
    ).reshape(row_count * clip_count * slot_count, text_width)
    keyvalue_flat = keyvalue_grad.reshape(row_count * clip_count * slot_count, 2 * width)
    keyvalue_weight_grad = left_tmul(context_slice, keyvalue_flat)
    context_grad = right_tmul(keyvalue_flat, keyvalue_back).astype(bf16)
    project_grad = left_tmul(text_slice, context_grad)
    bias_grad = jnp.sum(context_grad.astype(f32), axis=0)
    text_grad = right_tmul(context_grad, project_back).reshape(
        row_count, clip_count, slot_count, text_width
    )
    query_grad = left_tmul(normed_two, cross_queries_grad)
    normed_two_grad = right_tmul(cross_queries_grad, query_back)
    self_res_grad, gain_two_grad, shift_two_grad = norm_back(
        after_self, gain_two_b.astype(f32), shift_two_b.astype(f32), normed_two_grad
    )
    after_self_grad = after_cross_grad + self_res_grad
    self_branch_low = after_self_grad.astype(bf16)
    out_grad = left_tmul(attended_low, self_branch_low)
    attended_grad = (
        right_tmul(self_branch_low, out_back)
        .astype(bf16)
        .reshape(row_count, frame_count, head_count, head_size)
    )
    delta = jnp.einsum("rqhd,rhqd->rhq", attended_grad.astype(f32), attended)
    key_piece = lax.all_gather(keys_own, "seq", axis=1, tiled=True)
    value_piece = lax.all_gather(values_own, "seq", axis=1, tiled=True)
    count = key_piece.shape[1]
    key_heads = key_piece.reshape(row_count, count, head_count, head_size)
    value_heads = value_piece.reshape(row_count, count, head_count, head_size)
    scores = jnp.einsum("rqhd,rkhd->rhqk", queries, key_heads, preferred_element_type=f32) * scale
    allowed = visible(count)
    prob = jnp.where(allowed, jnp.exp(scores - log_total[..., None]), 0.0)
    prob_part = jnp.einsum(
        "rqhd,rkhd->rhqk", attended_grad, value_heads, preferred_element_type=f32
    )
    score_low = (prob * (prob_part - delta[..., None])).astype(bf16)
    query_acc = (
        jnp.einsum("rhqk,rkhd->rqhd", score_low, key_heads, preferred_element_type=f32) * scale
    )
    query_piece = lax.all_gather(
        queries.reshape(row_count, frame_count, width).astype(f32).astype(jnp.bfloat16),
        "seq",
        axis=1,
        tiled=True,
    ).astype(jnp.float32)
    grad_piece = lax.all_gather(
        attended_grad.reshape(row_count, frame_count, width).astype(f32).astype(jnp.bfloat16),
        "seq",
        axis=1,
        tiled=True,
    ).astype(jnp.float32)
    log_piece = lax.all_gather(
        log_total.transpose(0, 2, 1).astype(jnp.bfloat16), "seq", axis=1, tiled=True
    ).astype(jnp.float32)
    delta_piece = lax.all_gather(
        delta.transpose(0, 2, 1).astype(jnp.bfloat16), "seq", axis=1, tiled=True
    ).astype(jnp.float32)
    count = query_piece.shape[1]
    query_heads = query_piece.astype(bf16).reshape(row_count, count, head_count, head_size)
    grad_heads = grad_piece.astype(bf16).reshape(row_count, count, head_count, head_size)
    scores = (
        jnp.einsum("rqhd,rkhd->rhqk", query_heads, key_heads_own, preferred_element_type=f32)
        * scale
    )
    other_pos = jnp.arange(count, dtype=jnp.int32)
    causal = query_pos[None, None, :] <= other_pos[None, :, None]
    same_clip = segments[:, None, :] == all_segments[:, :, None]
    allowed = (causal & same_clip)[:, None]
    log_rows = log_piece.transpose(0, 2, 1)
    delta_rows = delta_piece.transpose(0, 2, 1)
    prob = jnp.where(allowed, jnp.exp(scores - log_rows[..., None]), 0.0)
    value_acc = jnp.einsum(
        "rhqk,rqhd->rkhd", prob.astype(bf16), grad_heads, preferred_element_type=f32
    )
    prob_part = jnp.einsum(
        "rqhd,rkhd->rhqk", grad_heads, value_heads_own, preferred_element_type=f32
    )
    score_low = (prob * (prob_part - delta_rows[..., None])).astype(bf16)
    key_acc = (
        jnp.einsum("rhqk,rqhd->rkhd", score_low, query_heads, preferred_element_type=f32) * scale
    )
    packed_grad = jnp.concatenate(
        [
            query_acc.reshape(token_count, width),
            key_acc.reshape(token_count, width),
            value_acc.reshape(token_count, width),
        ],
        axis=1,
    ).astype(bf16)
    qkv_grad = left_tmul(normed_one, packed_grad)
    normed_one_grad = right_tmul(packed_grad, qkv_back)
    input_res_grad, gain_one_grad, shift_one_grad = norm_back(
        inputs, gain_one_b.astype(f32), shift_one_b.astype(f32), normed_one_grad
    )
    frames_grad = (
        (after_self_grad + input_res_grad).astype(bf16).reshape(row_count, frame_count, width)
    )
    summed = (
        lax.psum_scatter(gain_one_grad, ("dp", "seq"), scatter_dimension=0, tiled=True),
        lax.psum_scatter(shift_one_grad, ("dp", "seq"), scatter_dimension=0, tiled=True),
        lax.psum_scatter(qkv_grad, ("dp", "seq"), scatter_dimension=0, tiled=True),
        lax.psum_scatter(out_grad, ("dp", "seq"), scatter_dimension=0, tiled=True),
        lax.psum_scatter(gain_two_grad, ("dp", "seq"), scatter_dimension=0, tiled=True),
        lax.psum_scatter(shift_two_grad, ("dp", "seq"), scatter_dimension=0, tiled=True),
        lax.psum_scatter(query_grad, ("dp", "seq"), scatter_dimension=0, tiled=True),
        lax.psum_scatter(project_grad, ("dp", "seq"), scatter_dimension=0, tiled=True),
        lax.psum_scatter(bias_grad, ("dp", "seq"), scatter_dimension=0, tiled=True),
        lax.psum_scatter(keyvalue_weight_grad, ("dp", "seq"), scatter_dimension=0, tiled=True),
        lax.psum_scatter(crossout_grad, ("dp", "seq"), scatter_dimension=0, tiled=True),
        lax.psum_scatter(gain_three_grad, ("dp", "seq"), scatter_dimension=0, tiled=True),
        lax.psum_scatter(shift_three_grad, ("dp", "seq"), scatter_dimension=0, tiled=True),
        lax.psum_scatter(feedin_grad, ("dp", "seq"), scatter_dimension=0, tiled=True),
        lax.psum_scatter(feedout_grad, ("dp", "seq"), scatter_dimension=0, tiled=True),
    )
    return (block_out, frames_grad, text_grad) + tuple(summed)


def solution(mesh):
    placed = (
        P("dp", "seq", None),
        P("dp", "seq"),
        P("dp", None, None, None),
        P("dp", None),
        P("dp", "seq", None),
        P(("dp", "seq")),
        P(("dp", "seq")),
        P(("dp", "seq"), None),
        P(("dp", "seq"), None),
        P(("dp", "seq")),
        P(("dp", "seq")),
        P(("dp", "seq"), None),
        P(("dp", "seq"), None),
        P(("dp", "seq")),
        P(("dp", "seq"), None),
        P(("dp", "seq"), None),
        P(("dp", "seq")),
        P(("dp", "seq")),
        P(("dp", "seq"), None),
        P(("dp", "seq"), None),
    )
    paired = mesh.shape["seq"] == 2 and mesh.shape["dp"] == 16
    return jax.shard_map(
        per_device_rows if paired else per_device,
        mesh=mesh,
        in_specs=placed,
        out_specs=(
            P("dp", "seq", None),
            P("dp", "seq", None),
            P("dp", None, "seq", None),
            P(("dp", "seq")),
            P(("dp", "seq")),
            P(("dp", "seq"), None),
            P(("dp", "seq"), None),
            P(("dp", "seq")),
            P(("dp", "seq")),
            P(("dp", "seq"), None),
            P(("dp", "seq"), None),
            P(("dp", "seq")),
            P(("dp", "seq"), None),
            P(("dp", "seq"), None),
            P(("dp", "seq")),
            P(("dp", "seq")),
            P(("dp", "seq"), None),
            P(("dp", "seq"), None),
        ),
        check_vma=False,
    )
```

```python
import functools

import jax
import jax.numpy as jnp
from jax import lax
from jax.experimental import pallas as pl
from jax.experimental.pallas import tpu as pltpu
from jax.sharding import PartitionSpec as P

HEADS = 16
HD = 64
PAIR = 2 * HD
epsilon = 1e-05
f32 = jnp.float32
bf16 = jnp.bfloat16
HIDE = 2.0 ** 50
MEG = 1024 * 1024


def dot_nn(a, b):
    return lax.dot_general(a, b, (((1,), (0,)), ((), ())), preferred_element_type=f32)


def dot_nt(a, b):
    return lax.dot_general(a, b, (((1,), (1,)), ((), ())), preferred_element_type=f32)


def dot_tn(a, b):
    return lax.dot_general(a, b, (((0,), (0,)), ((), ())), preferred_element_type=f32)


def norm_parts(x):
    mu = jnp.mean(x, axis=-1, keepdims=True)
    xc = x - mu
    rstd = lax.rsqrt(jnp.mean(xc * xc, axis=-1, keepdims=True) + epsilon)
    return xc * rstd, rstd


def norm_pull(n, rstd, gain, dy):
    dn = dy * gain
    dx = rstd * (
        dn - jnp.mean(dn, axis=-1, keepdims=True) - n * jnp.mean(dn * n, axis=-1, keepdims=True)
    )
    return dx


def params(mb, **kw):
    return pltpu.CompilerParams(vmem_limit_bytes=mb * MEG, **kw)


MESH = pl.DeviceIdType.MESH
ANY = pl.BlockSpec(memory_space=pl.ANY)


def whereabouts():
    at = lax.axis_index("dp")
    return {"z": at // 4, "y": lax.rem(at // 2, 2), "c": lax.rem(at, 2), "x": lax.axis_index("seq")}


def device(p):
    return (p["z"] * 4 + p["y"] * 2 + p["c"], p["x"])


def peers(pos, names):
    out = []
    for d in names:
        if d == "z":
            out += [dict(pos, z=lax.rem(pos["z"] + t, 4)) for t in (1, 2, 3)]
        else:
            out.append(dict(pos, **{d: 1 - pos[d]}))
    return out


def greet(pos):
    barrier = pltpu.get_barrier_semaphore()
    others = peers(pos, "zyxc")
    for p in others:
        pl.semaphore_signal(barrier, inc=1, device_id=device(p), device_id_type=MESH)
    pl.semaphore_wait(barrier, len(others))


class Gather:
    def __init__(self, src, out, sems, index, order, pos, rows=None, cols=None):
        self.send, self.recv, self.near = sems
        self.index, self.pos, self.out = index, pos, out
        self.tail = (slice(None) if rows is None else pl.ds(*rows), slice(None) if cols is None else pl.ds(*cols))
        self.src = src.at[self.tail]
        self.hops, self.stages = [], []
        done = ()
        for d in order + "c":
            here = []
            for t in (1, 2, 3) if d == "z" else (1,):
                if d == "z":
                    to = dict(pos, z=lax.rem(pos["z"] + t, 4))
                    fro = dict(pos, z=lax.rem(pos["z"] + 4 - t, 4))
                else:
                    to = fro = dict(pos, **{d: 1 - pos[d]})
                mine = self.region(done, pos)
                here.append(len(self.hops))
                self.hops.append((mine if done else self.src, mine, device(to), self.region(done, fro)))
            self.stages.append(here)
            done += (d,)
        self.last = len(self.stages)

    def region(self, done, p):
        return self.out.at[tuple(slice(None) if d in done else p[d] for d in "zycx") + self.tail]

    def copy(self, k, src, dst, to):
        return pltpu.make_async_remote_copy(
            src_ref=src, dst_ref=dst, send_sem=self.send.at[self.index, k], recv_sem=self.recv.at[self.index, k],
            device_id=to, device_id_type=MESH)

    def own(self):
        return pltpu.make_async_copy(self.src, self.region((), self.pos), self.near.at[self.index])

    def stage(self, n):
        if n == 0:
            self.own().start()
        if n == 1:
            self.own().wait()
        if n > 0:
            for k in self.stages[n - 1]:
                _, _, to, lands = self.hops[k]
                self.copy(k, lands, lands, to).wait_recv()
        if n < self.last:
            for k in self.stages[n]:
                src, dst, to, _ = self.hops[k]
                self.copy(k, src, dst, to).start()

    def finish(self):
        for k, (src, dst, to, _) in enumerate(self.hops):
            self.copy(k, src, dst, to).wait_send()


def gather_sems(n):
    return [pltpu.SemaphoreType.DMA((n, 6)), pltpu.SemaphoreType.DMA((n, 6)), pltpu.SemaphoreType.DMA((n,))]


GROUP = 4 * HD
SPLIT = 4


def attn_fwd_kernel(bq, frames_ref, aug_ref, vec_s, qkv_s, wo_s, wq_s, wkv_s, wc_s, wp_s,
                    x_out, augs_ref, vec_out, qkv_out, wo_out, wq_out, wkv_out, wc_out, wp_out,
                    a1_ref, q_ref, k_ref, v_ref, o_ref, lse_ref,
                    x_vm, vec_vm, w_vm, kx, vx, send, recv, near, sw_send, sw_recv, sw_near, ld_sem, w_sem):
    g = pl.program_id(0)
    n_tok, width = a1_ref.shape
    half_tok = n_tok // 2
    blocks = n_tok // bq
    pos = whereabouts()
    sems = (send, recv, near)
    chunk = 3 * GROUP
    qkv = [Gather(qkv_s, qkv_out, sems, i, "zxy" if i % 2 == 0 else "zyx", pos, cols=(i * chunk, chunk))
           for i in range(SPLIT)]
    vec = Gather(vec_s, vec_out, sems, 4, "zyx", pos)
    w_o = Gather(wo_s, wo_out, sems, 5, "zxy", pos)
    w_q = Gather(wq_s, wq_out, sems, 6, "zyx", pos)
    w_k = Gather(wkv_s, wkv_out, sems, 7, "zxy", pos, cols=(0, width))
    w_v = Gather(wkv_s, wkv_out, sems, 8, "zyx", pos, cols=(width, width))
    w_c = Gather(wc_s, wc_out, sems, 9, "zxy", pos)
    w_p = Gather(wp_s, wp_out, sems, 10, "zyx", pos)
    teams = [(vec, qkv[0], qkv[1]), (qkv[2], qkv[3]), (w_o, w_q), (w_k, w_v), (w_c, w_p)]

    def step(team, n):
        for member in teams[team]:
            member.stage(n)

    mine = pl.ds(pos["x"] * half_tok, half_tok)
    other = pl.ds((1 - pos["x"]) * half_tok, half_tok)
    across = device(dict(pos, x=1 - pos["x"]))

    def swaps(recv_side):
        rows = other if recv_side else mine
        out = []
        for i, (src, dst) in enumerate(((frames_ref, x_out), (aug_ref, augs_ref))):
            out.append(pltpu.make_async_remote_copy(
                src_ref=src.at[1 - pos["x"]], dst_ref=dst.at[rows], send_sem=sw_send.at[i], recv_sem=sw_recv.at[i],
                device_id=across, device_id_type=MESH))
        return out

    def keeps():
        return [pltpu.make_async_copy(src.at[pos["x"]], dst.at[mine], sw_near.at[i])
                for i, (src, dst) in enumerate(((frames_ref, x_out), (aug_ref, augs_ref)))]

    def weights(i):
        return pltpu.make_async_copy(
            qkv_out.at[:, :, :, :, :, pl.ds(i * chunk, chunk)], w_vm.at[i % 2], w_sem.at[i % 2])

    @pl.when(g == 0)
    def _():
        greet(pos)
        step(0, 0)
        for c in swaps(False):
            c.start()
        for c in keeps():
            c.start()
        step(1, 0)
        step(0, 1)
        step(2, 0)
        step(0, 2)
        step(1, 1)
        step(0, 3)
        step(1, 2)
        for c in keeps():
            c.wait()
        for c in swaps(True):
            c.wait_recv()
        loads = [pltpu.make_async_copy(x_out, x_vm, ld_sem.at[0]),
                 pltpu.make_async_copy(augs_ref.at[:, pl.ds(PAIR, PAIR)], kx.at[:, pl.ds(PAIR, PAIR)], ld_sem.at[1])]
        for c in loads:
            c.start()
        step(0, 4)
        weights(0).start()
        loads.append(pltpu.make_async_copy(vec_out, vec_vm, ld_sem.at[2]))
        loads[2].start()
        step(3, 0)
        step(2, 1)
        for c in loads:
            c.wait()
        lines = jnp.sum(vec_vm[...].astype(f32).reshape(8, 4, 16, 128), axis=1)
        gain = jnp.concatenate([lines[t, 0:1, :] for t in range(8)], axis=1)
        bias = jnp.concatenate([lines[t, 1:2, :] for t in range(8)], axis=1)

        @pl.loop(0, n_tok // 256)
        def _(i):
            rows = pl.ds(i * 256, 256)
            n, _ = norm_parts(x_vm[rows, :].astype(f32))
            a1_ref[rows, :] = (n * gain + bias).astype(bf16)

        vx[:, PAIR:] = jnp.ones((n_tok, PAIR), bf16)
        lse_ref[...] = jnp.zeros_like(lse_ref)

    def at(when, todo):
        @pl.when(g == when)
        def _():
            for t, n in todo:
                step(t, n)

    for i in range(SPLIT):
        @pl.when(g == i)
        def _():
            weights(i).wait()

    @pl.when(g == 0)
    def _():
        weights(1).start()

    w = w_vm.at[lax.rem(g, 2)]
    for i in range(3):
        rows = slice(i * 512, (i + 1) * 512)
        y = dot_nn(a1_ref[rows, :], w[...].reshape(width, chunk))
        q_ref[rows, :] = y[:, :GROUP].astype(bf16)
        k_ref[rows, :] = y[:, GROUP:2 * GROUP].astype(bf16)
        v_ref[rows, :] = y[:, 2 * GROUP:].astype(bf16)
    at(0, [(1, 3), (2, 2), (3, 1)])
    at(1, [(3, 2), (4, 1)])
    at(2, [(3, 4)])

    lane = lax.broadcasted_iota(jnp.int32, (bq, PAIR), 1)
    causal = lax.broadcasted_iota(jnp.int32, (bq, bq), 0) >= lax.broadcasted_iota(
        jnp.int32, (bq, bq), 1
    )
    for pair in range(2):
        cols = slice(pair * PAIR, (pair + 1) * PAIR)
        kx[:, :PAIR] = k_ref[:, cols]
        vx[:, :PAIR] = v_ref[:, cols]
        for i in range(blocks):
            rows = slice(i * bq, (i + 1) * bq)
            n = (i + 1) * bq
            q = q_ref[rows, cols] * bf16(HD ** -0.5)
            stat = lse_ref[rows, :]
            aq = (kx[rows, PAIR:] * bf16(1 / HIDE) - bf16(1.0)) * bf16(HIDE)
            aq = jnp.where(lane < 4, aq, bf16(0))
            outs = []
            for half in range(2):
                mine_l = (lane < HD) if half == 0 else (lane >= HD)
                qx = jnp.concatenate([jnp.where(mine_l, q, bf16(0)), aq], axis=1)
                s = dot_nt(qx, kx[:n, :])
                last = jnp.where(causal, s[:, n - bq:], -HIDE * HIDE)
                top = jnp.max(last, axis=1, keepdims=True)
                if i:
                    top = jnp.maximum(top, jnp.max(s[:, : n - bq], axis=1, keepdims=True))
                    p = jnp.concatenate(
                        [jnp.exp(s[:, : n - bq] - top).astype(bf16), jnp.exp(last - top).astype(bf16)],
                        axis=1,
                    )
                else:
                    p = jnp.exp(last - top).astype(bf16)
                o = dot_nn(p, vx[:n, :])
                total = o[:, PAIR:]
                outs.append(o[:, :PAIR] / total)
                stat = jnp.where(lane == 4 * g + 2 * pair + half, top + jnp.log(total), stat)
            o_ref[rows, cols] = jnp.where(lane < HD, outs[0], outs[1]).astype(bf16)
            lse_ref[rows, :] = stat
        if pair == 0:
            at(0, [(1, 4), (4, 0)])
            at(1, [(2, 3)])
            at(2, [(4, 2)])

    at(1, [(2, 4), (3, 3)])
    at(2, [(4, 3)])
    for i in range(1, SPLIT - 1):
        @pl.when(g == i)
        def _():
            weights(i + 1).start()

    @pl.when(g == SPLIT - 1)
    def _():
        step(4, 4)
        for team in teams:
            for member in team:
                member.finish()
        for c in swaps(False):
            c.wait_send()


def attn_fwd(frames, aug, vec_s, qkv_s, wo_s, wq_s, wkv_s, wc_s, wp_s, bq=512):
    halves, half_tok, width = frames.shape
    n_tok = 2 * half_tok
    whole = lambda shape: pl.BlockSpec(shape, lambda g: (0, 0))
    out_col = pl.BlockSpec((n_tok, GROUP), lambda g: (0, g))
    S = jax.ShapeDtypeStruct
    tall = S((n_tok, width), bf16)
    shards = [vec_s, qkv_s, wo_s, wq_s, wkv_s, wc_s, wp_s]
    return pl.pallas_call(
        functools.partial(attn_fwd_kernel, bq),
        grid=(SPLIT,),
        in_specs=[ANY] * 9,
        out_specs=[ANY] * 9 + [whole((n_tok, width)), out_col, out_col, out_col, out_col, whole((n_tok, PAIR))],
        out_shape=[tall, S((n_tok, 2 * PAIR), bf16)] + [S((4, 2, 2, 2) + s.shape, bf16) for s in shards]
        + [tall, tall, tall, tall, tall, S((n_tok, PAIR), f32)],
        scratch_shapes=[pltpu.VMEM((n_tok, width), bf16), pltpu.VMEM((4, 2, 2, 2, 16, 128), bf16),
                        pltpu.VMEM((2, 4, 2, 2, 2, width // 32, 3 * GROUP), bf16),
                        pltpu.VMEM((n_tok, 2 * PAIR), bf16), pltpu.VMEM((n_tok, 2 * PAIR), bf16)]
        + gather_sems(11) + [pltpu.SemaphoreType.DMA((2,))] * 3
        + [pltpu.SemaphoreType.DMA((3,)), pltpu.SemaphoreType.DMA((2,))],
        compiler_params=params(58, collective_id=0, has_side_effects=True),
        name="self_attention_fwd",
    )(frames, aug, *shards)


def cross_fwd_kernel(x_ref, o_ref, wo_ref, g2_ref, b2_ref, wq_ref, kc_ref, vc_ref, aq_ref, ac_ref,
                     wc_ref, g3_ref, b3_ref,
                     x1_ref, a2_ref, qc_ref, oc_ref, x2_ref, a3_ref):
    rows, width = x_ref.shape
    slots = kc_ref.shape[0]
    x1 = x_ref[...].astype(f32) + dot_nn(o_ref[...], wo_ref[...])
    x1_ref[...] = x1
    n, _ = norm_parts(x1)
    a2 = (n * g2_ref[...].astype(f32) + b2_ref[...].astype(f32)).astype(bf16)
    a2_ref[...] = a2
    qc_ref[...] = dot_nn(a2, wq_ref[...]).astype(bf16)
    lane = lax.broadcasted_iota(jnp.int32, (rows, PAIR), 1)
    ones = jnp.ones((slots, PAIR), bf16)
    for h in range(width // PAIR):
        cols = slice(h * PAIR, (h + 1) * PAIR)
        q = qc_ref[:, cols] * bf16(HD ** -0.5)
        kx = jnp.concatenate([kc_ref[:, cols], ac_ref[...]], axis=1)
        vx = jnp.concatenate([vc_ref[:, cols], ones], axis=1)
        outs = []
        for half in range(2):
            mine = (lane < HD) if half == 0 else (lane >= HD)
            qx = jnp.concatenate([jnp.where(mine, q, bf16(0)), aq_ref[...]], axis=1)
            s = dot_nt(qx, kx)
            p = jnp.exp(s - jnp.max(s, axis=1, keepdims=True)).astype(bf16)
            o = dot_nn(p, vx)
            outs.append(o[:, :PAIR] / o[:, PAIR:])
        oc_ref[:, cols] = jnp.where(lane < HD, outs[0], outs[1]).astype(bf16)
    x2 = x1 + dot_nn(oc_ref[...], wc_ref[...])
    x2_ref[...] = x2
    n, _ = norm_parts(x2)
    a3_ref[...] = (n * g3_ref[...].astype(f32) + b3_ref[...].astype(f32)).astype(bf16)


def cross_fwd(x, o, wo, g2, b2, wq, kvc, aug_q, aug_c, wc, g3, b3, rows=512):
    n_tok, width = x.shape
    slots = kvc.shape[0]
    tall = pl.BlockSpec((rows, width), lambda i: (i, 0))
    whole = lambda shape, j=0: pl.BlockSpec(shape, lambda i, j=j: (0, j))
    vec = whole((1, width))
    sq = whole((width, width))
    o16 = jax.ShapeDtypeStruct((n_tok, width), bf16)
    o32 = jax.ShapeDtypeStruct((n_tok, width), f32)
    return pl.pallas_call(
        cross_fwd_kernel,
        grid=(n_tok // rows,),
        in_specs=[tall, tall, sq, vec, vec, sq, whole((slots, width)), whole((slots, width), 1),
                  pl.BlockSpec((rows, PAIR), lambda i: (i, 0)), whole((slots, PAIR)), sq, vec, vec],
        out_specs=[tall] * 6,
        out_shape=[o32, o16, o16, o16, o32, o16],
        compiler_params=params(56),
        name="cross_attention_fwd",
    )(x, o, wo, g2, b2, wq, kvc, kvc, aug_q, aug_c, wc, g3, b3)


def gelu_and_slope(u):
    a = jnp.abs(u)
    t = 1.0 / (1.0 + (0.3275911 * 0.7071067811865476) * a)
    e = jnp.exp(-0.5 * (u * u))
    poly = t * (0.254829592 + t * (-0.284496736 + t * (1.421413741 + t * (-1.453152027 + t * 1.061405429))))
    tail = (0.5 * poly) * e
    phi = jnp.where(u >= 0, 1.0 - tail, tail)
    return u * phi, phi + u * (e * 0.3989422804014327)


def feed_kernel(rows, a3_ref, g_ref, x2_ref, gain_ref, bias_ref, wi_ref, wo_ref,
                out_ref, dx2_ref, gi_ref, go_ref, dgain_ref, dbias_ref, acc, da3, a3t, gl, du):
    c = pl.program_id(0)
    n_tok, width = a3_ref.shape
    blocks = n_tok // rows

    @pl.when(c == 0)
    def _():
        a3t[...] = a3_ref[...].T

    @pl.loop(0, blocks)
    def _(i):
        r = pl.ds(i * rows, rows)
        up = g_ref[r, :]
        u = dot_nn(a3_ref[r, :], wi_ref[...])
        act, slope = gelu_and_slope(u)
        act = act.astype(bf16)
        gl[r, :] = act
        y = dot_nn(act, wo_ref[...])
        d = (dot_nt(up, wo_ref[...]) * slope).astype(bf16)
        du[r, :] = d
        da = dot_nt(d, wi_ref[...])

        @pl.when(c == 0)
        def _():
            acc[r, :] = y
            da3[r, :] = da

        @pl.when(c > 0)
        def _():
            acc[r, :] += y
            da3[r, :] += da

    gi_ref[...] = dot_nn(a3t[...], du[...]).astype(bf16)
    go_ref[...] = dot_tn(gl[...], g_ref[...]).astype(bf16)

    @pl.when(c == pl.num_programs(0) - 1)
    def _():
        gain = gain_ref[...].astype(f32)
        dgain_ref[...] = jnp.zeros_like(dgain_ref)
        dbias_ref[...] = jnp.zeros_like(dbias_ref)

        @pl.loop(0, blocks * 2)
        def _(i):
            r = pl.ds(i * (rows // 2), rows // 2)
            x2 = x2_ref[r, :]
            out_ref[r, :] = (x2 + acc[r, :]).astype(bf16)
            n, rstd = norm_parts(x2)
            dy = da3[r, :]
            dx2_ref[r, :] = g_ref[r, :].astype(f32) + norm_pull(n, rstd, gain, dy)
            dgain_ref[...] += jnp.sum(dy * n, axis=0, keepdims=True)
            dbias_ref[...] += jnp.sum(dy, axis=0, keepdims=True)


def feed(a3, g, x2, gain, bias, w_in, w_out, rows=512, cols=512):
    n_tok, width = a3.shape
    hidden = w_in.shape[1]
    whole = lambda shape: pl.BlockSpec(shape, lambda c: (0, 0), pipeline_mode=pl.Buffered(1))
    out_whole = lambda shape: pl.BlockSpec(shape, lambda c: (0, 0))
    wi = pl.BlockSpec((width, cols), lambda c: (0, c))
    wo = pl.BlockSpec((cols, width), lambda c: (c, 0))
    S = jax.ShapeDtypeStruct
    return pl.pallas_call(
        functools.partial(feed_kernel, rows),
        grid=(hidden // cols,),
        in_specs=[whole((n_tok, width)), whole((n_tok, width)), whole((n_tok, width)),
                  whole((1, width)), whole((1, width)), wi, wo],
        out_specs=[whole((n_tok, width)), whole((n_tok, width)), wi, wo,
                   out_whole((1, width)), out_whole((1, width))],
        out_shape=[S((n_tok, width), bf16), S((n_tok, width), f32), S((width, hidden), bf16),
                   S((hidden, width), bf16), S((1, width), f32), S((1, width), f32)],
        scratch_shapes=[pltpu.VMEM((n_tok, width), f32), pltpu.VMEM((n_tok, width), f32),
                        pltpu.VMEM((width, n_tok), bf16), pltpu.VMEM((n_tok, cols), bf16),
                        pltpu.VMEM((n_tok, cols), bf16)],
        compiler_params=params(60),
        name="feed_forward_both",
    )(a3, g, x2, gain, bias, w_in, w_out)


def cross_bwd_kernel(dx2_ref, oc_ref, a2_ref, qc_ref, x1_ref, o_ref, aq_ref, ac_ref, kc_ref, vc_ref,
                     wc_ref, wq_ref, wo_ref, g2_ref, e_ref,
                     gc_ref, gq_ref, go_ref, dkv_ref, dx1_ref, do_ref, delta_ref, dgain_ref, dbias_ref,
                     acc_c, acc_q, acc_o, acc_kv, doc, dqc):
    i = pl.program_id(0)
    rows, width = dx2_ref.shape
    slots = kc_ref.shape[0]

    @pl.when(i == 0)
    def _():
        acc_c[...] = jnp.zeros_like(acc_c)
        acc_q[...] = jnp.zeros_like(acc_q)
        acc_o[...] = jnp.zeros_like(acc_o)
        acc_kv[...] = jnp.zeros_like(acc_kv)
        dgain_ref[...] = jnp.zeros_like(dgain_ref)
        dbias_ref[...] = jnp.zeros_like(dbias_ref)

    g2 = dx2_ref[...].astype(bf16)
    acc_c[...] += dot_tn(oc_ref[...], g2)
    doc[...] = dot_nt(g2, wc_ref[...]).astype(bf16)
    lane = lax.broadcasted_iota(jnp.int32, (rows, PAIR), 1)
    slot_lane = lax.broadcasted_iota(jnp.int32, (slots, PAIR), 1)
    ones = jnp.ones((slots, PAIR), bf16)
    for h in range(width // PAIR):
        cols = slice(h * PAIR, (h + 1) * PAIR)
        q = qc_ref[:, cols] * bf16(HD ** -0.5)
        up = doc[:, cols]
        k = kc_ref[:, cols]
        v = vc_ref[:, cols]
        kx = jnp.concatenate([k, ac_ref[...]], axis=1)
        dqs, dks, dvs = [], [], []
        for half in range(2):
            mine = (lane < HD) if half == 0 else (lane >= HD)
            qx = jnp.concatenate([jnp.where(mine, q, bf16(0)), aq_ref[...]], axis=1)
            s = dot_nt(qx, kx)
            w = jnp.exp(s - jnp.max(s, axis=1, keepdims=True))
            p = w / jnp.sum(w, axis=1, keepdims=True)
            dp = dot_nt(jnp.where(mine, up, bf16(0)), v)
            ds = (p * (dp - jnp.sum(dp * p, axis=1, keepdims=True))).astype(bf16)
            dqs.append(dot_nn(ds, k))
            dks.append(dot_tn(ds, q))
            dvs.append(dot_tn(p.astype(bf16), up))
        dqc[:, cols] = (jnp.where(lane < HD, dqs[0], dqs[1]) * (HD ** -0.5)).astype(bf16)
        acc_kv[:, cols] += jnp.where(slot_lane < HD, dks[0], dks[1])
        v_cols = slice(width + h * PAIR, width + (h + 1) * PAIR)
        acc_kv[:, v_cols] += jnp.where(slot_lane < HD, dvs[0], dvs[1])
    dq = dqc[...]
    acc_q[...] += dot_tn(a2_ref[...], dq)
    dy = dot_nt(dq, wq_ref[...])
    n, rstd = norm_parts(x1_ref[...])
    dgain_ref[...] += jnp.sum(dy * n, axis=0, keepdims=True)
    dbias_ref[...] += jnp.sum(dy, axis=0, keepdims=True)
    dx1 = dx2_ref[...] + norm_pull(n, rstd, g2_ref[...].astype(f32), dy)
    dx1_ref[...] = dx1
    g1 = dx1.astype(bf16)
    o = o_ref[...]
    acc_o[...] += dot_tn(o, g1)
    do = dot_nt(g1, wo_ref[...]).astype(bf16)
    do_ref[...] = do
    prod = do.astype(f32) * o.astype(f32)
    hi = prod.astype(bf16)
    lo = (prod - hi.astype(f32)).astype(bf16)
    delta_ref[...] = dot_nn(hi, e_ref[...]) + dot_nn(lo, e_ref[...])

    @pl.when(i == pl.num_programs(0) - 1)
    def _():
        gc_ref[...] = acc_c[...].astype(bf16)
        gq_ref[...] = acc_q[...].astype(bf16)
        go_ref[...] = acc_o[...].astype(bf16)
        dkv_ref[...] = acc_kv[...].astype(bf16)


def cross_bwd(dx2, oc, a2, qc, x1, o, aug_q, aug_c, kvc, wc, wq, wo, g2, head_sum, rows=256):
    n_tok, width = dx2.shape
    slots = kvc.shape[0]
    tall = pl.BlockSpec((rows, width), lambda i: (i, 0))
    thin = pl.BlockSpec((rows, PAIR), lambda i: (i, 0))
    whole = lambda shape, j=0: pl.BlockSpec(shape, lambda i, j=j: (0, j), pipeline_mode=pl.Buffered(1))
    once = lambda shape: pl.BlockSpec(shape, lambda i: (0, 0), pipeline_mode=pl.Buffered(1))
    out_vec = pl.BlockSpec((1, width), lambda i: (0, 0))
    sq = whole((width, width))
    S = jax.ShapeDtypeStruct
    return pl.pallas_call(
        cross_bwd_kernel,
        grid=(n_tok // rows,),
        in_specs=[tall, tall, tall, tall, tall, tall, thin, whole((slots, PAIR)),
                  whole((slots, width)), whole((slots, width), 1), sq, sq, sq, whole((1, width)),
                  whole((width, PAIR))],
        out_specs=[once((width, width))] * 3 + [once((slots, 2 * width)), tall, tall, thin, out_vec, out_vec],
        out_shape=[S((width, width), bf16)] * 3 + [
            S((slots, 2 * width), bf16), S((n_tok, width), f32), S((n_tok, width), bf16),
            S((n_tok, PAIR), f32), S((1, width), f32), S((1, width), f32)],
        scratch_shapes=[pltpu.VMEM((width, width), f32)] * 3 + [
            pltpu.VMEM((slots, 2 * width), f32), pltpu.VMEM((rows, width), bf16),
            pltpu.VMEM((rows, width), bf16)],
        compiler_params=params(60),
        name="cross_attention_bwd",
    )(dx2, oc, a2, qc, x1, o, aug_q, aug_c, kvc, kvc, wc, wq, wo, g2, head_sum)


def three_parts(v):
    hi = v.astype(bf16)
    rest = v - hi.astype(f32)
    mid = rest.astype(bf16)
    return hi, mid, (rest - mid.astype(f32)).astype(bf16)


def attn_bwd_kernel(bk, q_ref, k_ref, v_ref, do_ref, lse_ref, delta_ref, aq_ref, ak_ref, a1_ref, x_ref,
                    dx1_ref, gain_ref, wq_ref, wk_ref, wv_ref,
                    gq_ref, gk_ref, gv_ref, dx_ref, dgain_ref, dbias_ref,
                    a1t, da1, qx, dox, dq, dkv):
    h = pl.program_id(0)
    n_tok, width = a1_ref.shape
    blocks = n_tok // bk

    @pl.when(h == 0)
    def _():
        a1t[...] = a1_ref[...].T
        da1[...] = jnp.zeros_like(da1)

    lane = lax.broadcasted_iota(jnp.int32, (n_tok, PAIR), 1)
    lane_k = lax.broadcasted_iota(jnp.int32, (bk, PAIR), 1)
    causal = lax.broadcasted_iota(jnp.int32, (bk, bk), 0) <= lax.broadcasted_iota(
        jnp.int32, (bk, bk), 1
    )
    q = q_ref[...] * bf16(HD ** -0.5)
    up = do_ref[...]
    for half in range(2):
        mine = (lane < HD) if half == 0 else (lane >= HD)
        col = lane == 2 * h + half
        lse = jnp.sum(jnp.where(col, lse_ref[...], 0.0), axis=1, keepdims=True)
        dlt = jnp.sum(jnp.where(col, delta_ref[...], 0.0), axis=1, keepdims=True)
        l_hi, l_mid, l_lo = three_parts(jnp.broadcast_to(-lse, (n_tok, PAIR)))
        d_hi, d_mid, d_lo = three_parts(jnp.broadcast_to(-dlt, (n_tok, PAIR)))
        zero = jnp.zeros((n_tok, PAIR), bf16)

        def place(base, hi, mid, lo):
            return jnp.where(lane == 8, hi, jnp.where(lane == 9, mid, jnp.where(lane == 10, lo, base)))

        qx[:, :PAIR] = jnp.where(mine, q, bf16(0))
        qx[:, PAIR:] = place(aq_ref[...], l_hi, l_mid, l_lo)
        dox[:, :PAIR] = jnp.where(mine, up, bf16(0))
        dox[:, PAIR:] = place(zero, d_hi, d_mid, d_lo)
        unit = ((lane_k >= 8) & (lane_k <= 10)).astype(bf16)
        for j in range(blocks):
            rows = slice(j * bk, (j + 1) * bk)
            rest = slice(j * bk, n_tok)
            k = k_ref[rows, :]
            s = dot_nt(jnp.concatenate([k, ak_ref[rows, :] + unit], axis=1), qx[rest, :])
            head = jnp.where(causal, s[:, :bk], -HIDE * HIDE)
            s = jnp.concatenate([head, s[:, bk:]], axis=1) if j < blocks - 1 else head
            p = jnp.exp(s)
            dp = dot_nt(jnp.concatenate([v_ref[rows, :], unit], axis=1), dox[rest, :])
            ds = (p * dp).astype(bf16)
            dv = dot_nn(p.astype(bf16), dox[rest, :PAIR])
            dk = dot_nn(ds, qx[rest, :PAIR])
            if half == 0:
                dkv[rows, :PAIR] = dk
                dkv[rows, PAIR:] = dv
            else:
                dkv[rows, :PAIR] += dk
                dkv[rows, PAIR:] += dv
            part = dot_tn(ds, k)
            keep = (lane[rest, :] < HD) if half == 0 else (lane[rest, :] >= HD)
            part = jnp.where(keep, part, 0.0)
            if half == 0 and j == 0:
                dq[...] = part
            else:
                dq[rest, :] += part
    dq16 = (dq[...] * (HD ** -0.5)).astype(bf16)
    dk16 = dkv[:, :PAIR].astype(bf16)
    dv16 = dkv[:, PAIR:].astype(bf16)
    gq_ref[...] = dot_nn(a1t[...], dq16).astype(bf16)
    gk_ref[...] = dot_nn(a1t[...], dk16).astype(bf16)
    gv_ref[...] = dot_nn(a1t[...], dv16).astype(bf16)
    d3 = jnp.concatenate([dq16, dk16, dv16], axis=1)
    w3 = jnp.concatenate([wq_ref[...], wk_ref[...], wv_ref[...]], axis=1)
    da1[...] += dot_nt(d3, w3)

    @pl.when(h == pl.num_programs(0) - 1)
    def _():
        gain = gain_ref[...].astype(f32)
        dgain_ref[...] = jnp.zeros_like(dgain_ref)
        dbias_ref[...] = jnp.zeros_like(dbias_ref)

        @pl.loop(0, blocks)
        def _(i):
            r = pl.ds(i * bk, bk)
            n, rstd = norm_parts(x_ref[r, :].astype(f32))
            dy = da1[r, :]
            dx_ref[r, :] = (dx1_ref[r, :] + norm_pull(n, rstd, gain, dy)).astype(bf16)
            dgain_ref[...] += jnp.sum(dy * n, axis=0, keepdims=True)
            dbias_ref[...] += jnp.sum(dy, axis=0, keepdims=True)


def attn_bwd(q, k, v, do, lse, delta, augs, a1, x, dx1, gain, w_qkv, bk=256):
    n_tok, width = x.shape
    pairs = width // PAIR
    whole = lambda shape: pl.BlockSpec(shape, lambda h: (0, 0), pipeline_mode=pl.Buffered(1))
    vec = pl.BlockSpec((1, width), lambda h: (0, 0))
    tall = pl.BlockSpec((n_tok, PAIR), lambda h: (0, h))
    wcol = lambda off: pl.BlockSpec((width, PAIR), lambda h, off=off: (0, (h // 2) * 6 + off * 2 + h % 2))
    gcol = pl.BlockSpec((width, PAIR), lambda h: (0, h))
    S = jax.ShapeDtypeStruct
    return pl.pallas_call(
        functools.partial(attn_bwd_kernel, bk),
        grid=(pairs,),
        in_specs=[tall, tall, tall, tall, whole((n_tok, PAIR)), whole((n_tok, PAIR)),
                  whole((n_tok, PAIR)), pl.BlockSpec((n_tok, PAIR), lambda h: (0, 1)), whole((n_tok, width)),
                  whole((n_tok, width)), whole((n_tok, width)), vec, wcol(0), wcol(1), wcol(2)],
        out_specs=[gcol, gcol, gcol, whole((n_tok, width)), vec, vec],
        out_shape=[S((width, width), bf16)] * 3 + [S((n_tok, width), bf16), S((1, width), f32), S((1, width), f32)],
        scratch_shapes=[pltpu.VMEM((width, n_tok), bf16), pltpu.VMEM((n_tok, width), f32),
                        pltpu.VMEM((n_tok, 2 * PAIR), bf16), pltpu.VMEM((n_tok, 2 * PAIR), bf16),
                        pltpu.VMEM((n_tok, PAIR), f32), pltpu.VMEM((n_tok, 2 * PAIR), f32)],
        compiler_params=params(60),
        name="self_attention_bwd",
    )(q, k, v, do, lse, delta, augs, augs, a1, x, dx1, gain, w_qkv, w_qkv, w_qkv)


def spread_sum(part, order, steps):
    at = lax.axis_index("dp")
    place = {"z": at // 4, "y": (at // 2) % 2, "c": at % 2, "x": lax.axis_index("seq")}
    names = ["z", "y", "c", "x"]
    for step in order:
        name = step[0]
        axis = names.index(name)
        size = part.shape[axis]
        if name == "x":
            pairs, mesh_axis = [(0, 1), (1, 0)], "seq"
            mine = place["x"]
        else:
            flip = {"y": 2, "c": 1, "zh": 8, "zl": 4}[step]
            pairs, mesh_axis = [(i, i ^ flip) for i in range(16)], "dp"
            mine = {"y": place["y"], "c": place["c"], "zh": place["z"] // 2, "zl": place["z"] % 2}[step]
        half = size // 2
        keep = lax.dynamic_slice_in_dim(part, mine * half, half, axis)
        give = lax.dynamic_slice_in_dim(part, (1 - mine) * half, half, axis)
        got = lax.ppermute(give, mesh_axis, pairs)
        part = (keep.astype(f32) + got.astype(f32)).astype(bf16)
    return part.reshape(part.shape[4:]).astype(f32)


def per_device_rows(
    frames, segments, text_states, text_lengths, cotangent,
    self_norm_gain, self_norm_bias, self_qkv, self_output,
    cross_norm_gain, cross_norm_bias, cross_query, text_project, text_bias,
    cross_keyvalue, cross_output, feed_norm_gain, feed_norm_bias, feed_in, feed_out,
):
    at = lax.axis_index("seq")
    _, half, width = frames.shape
    n_tok = 2 * half
    everywhere = ("dp", "seq")
    flip = [(0, 1), (1, 0)]

    def swap_in(v):
        mine = lax.dynamic_index_in_dim(v, at, 0, keepdims=False)
        got = lax.ppermute(lax.dynamic_index_in_dim(v, 1 - at, 0, keepdims=False), "seq", flip)
        return jnp.where(at == 0, jnp.concatenate([mine, got]), jnp.concatenate([got, mine]))

    def swap_out(v):
        mine = lax.dynamic_slice_in_dim(v, at * half, half, 0)
        got = lax.ppermute(lax.dynamic_slice_in_dim(v, (1 - at) * half, half, 0), "seq", flip)
        return jnp.where(at == 0, jnp.stack([mine, got]), jnp.stack([got, mine]))

    gather = lambda v: lax.all_gather(v, everywhere, axis=0, tiled=True)
    number = lax.axis_index("dp") * 2 + at
    lane = jnp.arange(PAIR, dtype=jnp.int32)[None, :]
    vectors = jnp.stack([self_norm_gain, self_norm_bias, cross_norm_gain, cross_norm_bias,
                         text_bias, feed_norm_gain, feed_norm_bias])
    vectors = jnp.where(lane // 32 == number % 4, jnp.tile(jnp.pad(vectors, ((0, 9), (0, 0))), (1, 4)), bf16(0))

    segs = segments[:, :, None]
    lanes2 = jnp.arange(2 * PAIR, dtype=jnp.int32)[None, None, :]
    aug = jnp.where(
        lanes2 < PAIR, jnp.where(lanes2 == segs, -HIDE, 0.0),
        jnp.where((lanes2 < PAIR + 4) & (lanes2 - PAIR != segs), HIDE, 0.0)).astype(bf16)
    qkv_group = self_qkv.reshape(-1, 3, SPLIT, GROUP).transpose(0, 2, 1, 3).reshape(-1, 3 * width)

    (x, augs, vec_all, w_qkv, w_o, w_q, w_kv, w_c, w_p, a1, q, k, v, o, lse) = attn_fwd(
        frames, aug, vectors, qkv_group, self_output, cross_query, cross_keyvalue, cross_output,
        text_project.reshape(-1, width // 2))
    vec_all = jnp.sum(vec_all.reshape(8, 4, 16, 128).astype(f32), axis=1).transpose(1, 0, 2).reshape(16, width)
    vec = lambda i: vec_all[i][None, :]
    w_qkv, w_o, w_q, w_kv, w_c = [w.reshape(width, -1) for w in (w_qkv, w_o, w_q, w_kv, w_c)]
    w_p = w_p.reshape(-1, width)
    w_i = gather(feed_in)
    w_f = gather(feed_out)
    up = swap_in(cotangent)

    clips, txt, text_width = text_states.shape[1:]
    slots = clips * txt
    lengths = lax.dynamic_index_in_dim(text_lengths, at, 0, keepdims=False)
    slot = jnp.arange(slots, dtype=jnp.int32)
    live = (slot % txt) < jnp.repeat(lengths, txt)
    aug_c = jnp.where((lane < 4) & ~((lane == (slot // txt)[:, None]) & live[:, None]), HIDE, 0.0).astype(bf16)

    text = lax.dynamic_index_in_dim(text_states, at, 0, keepdims=False).reshape(slots, text_width)
    context = (dot_nn(text, w_p) + vec(4).astype(f32)).astype(bf16)
    kvc = dot_nn(context, w_kv).astype(bf16)
    x1, a2, qc, oc, x2, a3 = cross_fwd(x, o, w_o, vec(2), vec(3), w_q, kvc, augs, aug_c, w_c, vec(5), vec(6))

    block_out, dx2, g_i, g_f, dgain3, dbias3 = feed(a3, up, x2, vec(5), vec(6), w_i, w_f)

    head_sum = (jnp.arange(width, dtype=jnp.int32)[:, None] // HD == lane).astype(bf16)
    g_c, g_q, g_o, dkv, dx1, do, delta, dgain2, dbias2 = cross_bwd(
        dx2, oc, a2, qc, x1, o, augs, aug_c, kvc, w_c, w_q, w_o, vec(2), head_sum)

    g_kv = dot_tn(context, dkv).astype(bf16)
    dc = dot_nt(dkv, w_kv).astype(bf16)
    g_p = dot_tn(text, dc).astype(bf16)
    dbias_t = jnp.sum(dc.astype(f32), axis=0)
    text_grad = dot_nt(dc, w_p).reshape(clips, txt, text_width)
    th = txt // 2
    t_mine = lax.dynamic_slice_in_dim(text_grad, at * th, th, 1)
    t_got = lax.ppermute(lax.dynamic_slice_in_dim(text_grad, (1 - at) * th, th, 1), "seq", flip)
    text_out = jnp.where(at == 0, jnp.stack([t_mine, t_got]), jnp.stack([t_got, t_mine]))

    g_wq, g_wk, g_wv, dx, dgain1, dbias1 = attn_bwd(
        q, k, v, do, lse, delta, augs, a1, x, dx1, vec(0), w_qkv)

    def total(g, order):
        rows = g.shape[0] // 32
        return spread_sum(g.reshape((4, 2, 2, 2, rows) + g.shape[1:]), order, None)

    xy = ["c", "x", "y", "zh", "zl"]
    yx = ["c", "y", "x", "zh", "zl"]
    s_i = total(g_i, xy)
    s_f = total(g_f, yx)
    s_c = total(g_c, xy)
    s_q = total(g_q, yx)
    s_o = total(g_o, xy)
    s_kv = total(g_kv, yx)
    s_p = total(g_p, xy)
    s_wq = total(g_wq, xy)
    s_wk = total(g_wk, yx)
    s_wv = total(g_wv, xy)
    s_qkv = jnp.concatenate([s_wq, s_wk, s_wv], axis=1)
    vecs = jnp.concatenate([dgain1, dbias1, dgain2, dbias2, dbias_t[None, :], dgain3, dbias3])
    vecs = lax.psum_scatter(vecs, everywhere, scatter_dimension=1, tiled=True)
    return (
        swap_out(block_out), swap_out(dx), text_out, vecs[0], vecs[1], s_qkv, s_o, vecs[2], vecs[3],
        s_q, s_p, vecs[4], s_kv, s_c, vecs[5], vecs[6], s_i, s_f,
    )


big_negative = -1e30


def layer_norm(values, gain, shift):
    centre = jnp.mean(values, axis=-1, keepdims=True)
    centred = values - centre
    spread = jnp.mean(centred * centred, axis=-1, keepdims=True)
    return centred * lax.rsqrt(spread + epsilon) * gain + shift


def norm_back(values, gain, shift, upstream):
    _, pull = jax.vjp(layer_norm, values, gain, shift)
    return pull(upstream)


def gelu_exact(values):
    return jax.nn.gelu(values, approximate=False)


def matmul(left, right):
    return jnp.dot(left, right, preferred_element_type=jnp.float32)


def left_tmul(left, right):
    return lax.dot_general(
        left, right, (((0,), (0,)), ((), ())), preferred_element_type=jnp.float32
    )


def right_tmul(left, right):
    return lax.dot_general(
        left, right, (((1,), (1,)), ((), ())), preferred_element_type=jnp.float32
    )


def per_device(
    frames,
    segments,
    text_states,
    text_lengths,
    cotangent,
    self_norm_gain,
    self_norm_bias,
    self_qkv,
    self_output,
    cross_norm_gain,
    cross_norm_bias,
    cross_query,
    text_project,
    text_bias,
    cross_keyvalue,
    cross_output,
    feed_norm_gain,
    feed_norm_bias,
    feed_in,
    feed_out,
):
    shards = (
        self_norm_gain,
        self_norm_bias,
        self_qkv,
        self_output,
        cross_norm_gain,
        cross_norm_bias,
        cross_query,
        text_project,
        text_bias,
        cross_keyvalue,
        cross_output,
        feed_norm_gain,
        feed_norm_bias,
        feed_in,
        feed_out,
    )
    gathered = (
        lax.all_gather(shards[0], ("dp", "seq"), axis=0, tiled=True),
        lax.all_gather(shards[1], ("dp", "seq"), axis=0, tiled=True),
        lax.all_gather(shards[2], ("dp", "seq"), axis=0, tiled=True),
        lax.all_gather(shards[3], ("dp", "seq"), axis=0, tiled=True),
        lax.all_gather(shards[4], ("dp", "seq"), axis=0, tiled=True),
        lax.all_gather(shards[5], ("dp", "seq"), axis=0, tiled=True),
        lax.all_gather(shards[6], ("dp", "seq"), axis=0, tiled=True),
        lax.all_gather(shards[7], ("dp", "seq"), axis=0, tiled=True),
        lax.all_gather(shards[8], ("dp", "seq"), axis=0, tiled=True),
        lax.all_gather(shards[9], ("dp", "seq"), axis=0, tiled=True),
        lax.all_gather(shards[10], ("dp", "seq"), axis=0, tiled=True),
        lax.all_gather(shards[11], ("dp", "seq"), axis=0, tiled=True),
        lax.all_gather(shards[12], ("dp", "seq"), axis=0, tiled=True),
        lax.all_gather(shards[13], ("dp", "seq"), axis=0, tiled=True),
        lax.all_gather(shards[14], ("dp", "seq"), axis=0, tiled=True),
    )
    (
        gain_one,
        shift_one,
        qkv_full,
        out_full,
        gain_two,
        shift_two,
        query_full,
        project_full,
        bias_full,
        keyvalue_full,
        crossout_full,
        gain_three,
        shift_three,
        feedin_full,
        feedout_full,
    ) = gathered
    f32 = jnp.float32
    bf16 = jnp.bfloat16
    row_count, frame_count, width = frames.shape
    token_count = row_count * frame_count
    head_count = HEADS
    head_size = HD
    scale = head_size ** (-0.5)
    seq_index = lax.axis_index("seq")
    query_pos = seq_index * frame_count + jnp.arange(frame_count, dtype=jnp.int32)
    all_segments = lax.all_gather(segments, "seq", axis=1, tiled=True)

    def visible(count):
        key_pos = jnp.arange(count, dtype=jnp.int32)
        causal = key_pos[None, None, :] <= query_pos[None, :, None]
        same_clip = all_segments[:, None, :] == segments[:, :, None]
        return (causal & same_clip)[:, None]

    inputs = frames.astype(f32).reshape(token_count, width)
    normed_one = layer_norm(inputs, gain_one.astype(f32), shift_one.astype(f32)).astype(bf16)
    packed = matmul(normed_one, qkv_full).astype(bf16)
    queries = packed[:, :width].reshape(row_count, frame_count, head_count, head_size)
    keys_own = packed[:, width : 2 * width].reshape(row_count, frame_count, width)
    values_own = packed[:, 2 * width :].reshape(row_count, frame_count, width)
    key_heads_own = keys_own.reshape(row_count, frame_count, head_count, head_size)
    value_heads_own = values_own.reshape(row_count, frame_count, head_count, head_size)
    running = jnp.full((row_count, head_count, frame_count), big_negative, f32)
    key_piece = lax.all_gather(keys_own, "seq", axis=1, tiled=True)
    value_piece = lax.all_gather(values_own, "seq", axis=1, tiled=True)
    count = key_piece.shape[1]
    key_heads = key_piece.reshape(row_count, count, head_count, head_size)
    value_heads = value_piece.reshape(row_count, count, head_count, head_size)
    scores = jnp.einsum("rqhd,rkhd->rhqk", queries, key_heads, preferred_element_type=f32) * scale
    allowed = visible(count)
    masked = jnp.where(allowed, scores, big_negative)
    fresh = jnp.maximum(running, jnp.max(masked, axis=-1))
    weights = jnp.where(allowed, jnp.exp(masked - fresh[..., None]), 0.0)
    total = jnp.sum(weights, axis=-1)
    accum = jnp.einsum(
        "rhqk,rkhd->rhqd", weights.astype(bf16), value_heads, preferred_element_type=f32
    )
    running, total, accum = (fresh, total, accum)
    attended = accum / total[..., None]
    log_total = running + jnp.log(total)
    attended_low = attended.transpose(0, 2, 1, 3).reshape(token_count, width).astype(bf16)
    after_self = inputs + matmul(attended_low, out_full)
    normed_two = layer_norm(after_self, gain_two.astype(f32), shift_two.astype(f32)).astype(bf16)
    cross_queries = (
        matmul(normed_two, query_full)
        .astype(bf16)
        .reshape(row_count, frame_count, head_count, head_size)
    )
    clip_count, text_count, text_width = text_states.shape[1:]
    slot_total = clip_count * text_count
    text_flat = text_states.reshape(row_count * slot_total, text_width)
    context = (matmul(text_flat, project_full) + bias_full.astype(f32)).astype(bf16)
    keyvalue = matmul(context, keyvalue_full).astype(bf16).reshape(row_count, slot_total, 2 * width)
    cross_keys = keyvalue[..., :width].reshape(row_count, slot_total, head_count, head_size)
    cross_values = keyvalue[..., width:].reshape(row_count, slot_total, head_count, head_size)
    slot_ids = jnp.arange(slot_total, dtype=jnp.int32)
    key_clip = slot_ids // text_count
    key_slot = slot_ids % text_count
    live = key_slot[None, :] < jnp.repeat(text_lengths, text_count, axis=1)
    cross_allowed = ((segments[:, :, None] == key_clip[None, None, :]) & live[:, None, :])[:, None]
    cross_scores = (
        jnp.einsum("rqhd,rkhd->rhqk", cross_queries, cross_keys, preferred_element_type=f32) * scale
    )
    cross_masked = jnp.where(cross_allowed, cross_scores, big_negative)
    cross_top = jnp.max(cross_masked, axis=-1, keepdims=True)
    cross_weights = jnp.where(cross_allowed, jnp.exp(cross_masked - cross_top), 0.0)
    cross_prob = cross_weights / jnp.sum(cross_weights, axis=-1, keepdims=True)
    cross_low = cross_prob.astype(bf16)
    cross_mixed = jnp.einsum("rhqk,rkhd->rqhd", cross_low, cross_values, preferred_element_type=f32)
    cross_mixed_low = cross_mixed.reshape(token_count, width).astype(bf16)
    after_cross = after_self + matmul(cross_mixed_low, crossout_full)
    normed_three = layer_norm(after_cross, gain_three.astype(f32), shift_three.astype(f32)).astype(
        bf16
    )
    hidden_pre = matmul(normed_three, feedin_full)
    hidden_low = gelu_exact(hidden_pre).astype(bf16)
    result = after_cross + matmul(hidden_low, feedout_full)
    block_out = result.astype(bf16).reshape(row_count, frame_count, width)
    regathered = (
        lax.all_gather(shards[0], ("dp", "seq"), axis=0, tiled=True),
        lax.all_gather(shards[1], ("dp", "seq"), axis=0, tiled=True),
        lax.all_gather(shards[2], ("dp", "seq"), axis=0, tiled=True),
        lax.all_gather(shards[3], ("dp", "seq"), axis=0, tiled=True),
        lax.all_gather(shards[4], ("dp", "seq"), axis=0, tiled=True),
        lax.all_gather(shards[5], ("dp", "seq"), axis=0, tiled=True),
        lax.all_gather(shards[6], ("dp", "seq"), axis=0, tiled=True),
        lax.all_gather(shards[7], ("dp", "seq"), axis=0, tiled=True),
        lax.all_gather(shards[8], ("dp", "seq"), axis=0, tiled=True),
        lax.all_gather(shards[9], ("dp", "seq"), axis=0, tiled=True),
        lax.all_gather(shards[10], ("dp", "seq"), axis=0, tiled=True),
        lax.all_gather(shards[11], ("dp", "seq"), axis=0, tiled=True),
        lax.all_gather(shards[12], ("dp", "seq"), axis=0, tiled=True),
        lax.all_gather(shards[13], ("dp", "seq"), axis=0, tiled=True),
        lax.all_gather(shards[14], ("dp", "seq"), axis=0, tiled=True),
    )
    (
        gain_one_b,
        shift_one_b,
        qkv_back,
        out_back,
        gain_two_b,
        shift_two_b,
        query_back,
        project_back,
        bias_back,
        keyvalue_back,
        crossout_back,
        gain_three_b,
        shift_three_b,
        feedin_back,
        feedout_back,
    ) = regathered
    upstream = cotangent.astype(f32).reshape(token_count, width)
    upstream_low = cotangent.reshape(token_count, width)
    feedout_grad = left_tmul(hidden_low, upstream_low)
    hidden_grad = right_tmul(upstream_low, feedout_back)
    _, gelu_pull = jax.vjp(gelu_exact, hidden_pre)
    (pre_grad,) = gelu_pull(hidden_grad)
    pre_grad_low = pre_grad.astype(bf16)
    feedin_grad = left_tmul(normed_three, pre_grad_low)
    normed_three_grad = right_tmul(pre_grad_low, feedin_back)
    cross_res_grad, gain_three_grad, shift_three_grad = norm_back(
        after_cross, gain_three_b.astype(f32), shift_three_b.astype(f32), normed_three_grad
    )
    after_cross_grad = upstream + cross_res_grad
    cross_branch_low = after_cross_grad.astype(bf16)
    crossout_grad = left_tmul(cross_mixed_low, cross_branch_low)
    mixed_grad = (
        right_tmul(cross_branch_low, crossout_back)
        .astype(bf16)
        .reshape(row_count, frame_count, head_count, head_size)
    )
    prob_grad = jnp.einsum("rqhd,rkhd->rhqk", mixed_grad, cross_values, preferred_element_type=f32)
    cross_values_grad = jnp.einsum(
        "rhqk,rqhd->rkhd", cross_low, mixed_grad, preferred_element_type=f32
    )
    cross_score_low = (
        cross_prob * (prob_grad - jnp.sum(prob_grad * cross_prob, axis=-1, keepdims=True))
    ).astype(bf16)
    cross_queries_grad = (
        (
            jnp.einsum("rhqk,rkhd->rqhd", cross_score_low, cross_keys, preferred_element_type=f32)
            * scale
        )
        .astype(bf16)
        .reshape(token_count, width)
    )
    cross_keys_grad = (
        jnp.einsum("rhqk,rqhd->rkhd", cross_score_low, cross_queries, preferred_element_type=f32)
        * scale
    )
    keyvalue_part = jnp.concatenate(
        [
            cross_keys_grad.reshape(row_count, clip_count, text_count, width),
            cross_values_grad.reshape(row_count, clip_count, text_count, width),
        ],
        axis=3,
    )
    keyvalue_grad = (
        lax.psum_scatter(keyvalue_part.astype(jnp.bfloat16), "seq", scatter_dimension=2, tiled=True)
        .astype(jnp.float32)
        .astype(bf16)
    )
    slot_count = keyvalue_grad.shape[2]
    context_slice = lax.dynamic_slice_in_dim(
        context.reshape(row_count, clip_count, text_count, width),
        seq_index * slot_count,
        slot_count,
        2,
    ).reshape(row_count * clip_count * slot_count, width)
    text_slice = lax.dynamic_slice_in_dim(
        text_states, seq_index * slot_count, slot_count, 2
    ).reshape(row_count * clip_count * slot_count, text_width)
    keyvalue_flat = keyvalue_grad.reshape(row_count * clip_count * slot_count, 2 * width)
    keyvalue_weight_grad = left_tmul(context_slice, keyvalue_flat)
    context_grad = right_tmul(keyvalue_flat, keyvalue_back).astype(bf16)
    project_grad = left_tmul(text_slice, context_grad)
    bias_grad = jnp.sum(context_grad.astype(f32), axis=0)
    text_grad = right_tmul(context_grad, project_back).reshape(
        row_count, clip_count, slot_count, text_width
    )
    query_grad = left_tmul(normed_two, cross_queries_grad)
    normed_two_grad = right_tmul(cross_queries_grad, query_back)
    self_res_grad, gain_two_grad, shift_two_grad = norm_back(
        after_self, gain_two_b.astype(f32), shift_two_b.astype(f32), normed_two_grad
    )
    after_self_grad = after_cross_grad + self_res_grad
    self_branch_low = after_self_grad.astype(bf16)
    out_grad = left_tmul(attended_low, self_branch_low)
    attended_grad = (
        right_tmul(self_branch_low, out_back)
        .astype(bf16)
        .reshape(row_count, frame_count, head_count, head_size)
    )
    delta = jnp.einsum("rqhd,rhqd->rhq", attended_grad.astype(f32), attended)
    key_piece = lax.all_gather(keys_own, "seq", axis=1, tiled=True)
    value_piece = lax.all_gather(values_own, "seq", axis=1, tiled=True)
    count = key_piece.shape[1]
    key_heads = key_piece.reshape(row_count, count, head_count, head_size)
    value_heads = value_piece.reshape(row_count, count, head_count, head_size)
    scores = jnp.einsum("rqhd,rkhd->rhqk", queries, key_heads, preferred_element_type=f32) * scale
    allowed = visible(count)
    prob = jnp.where(allowed, jnp.exp(scores - log_total[..., None]), 0.0)
    prob_part = jnp.einsum(
        "rqhd,rkhd->rhqk", attended_grad, value_heads, preferred_element_type=f32
    )
    score_low = (prob * (prob_part - delta[..., None])).astype(bf16)
    query_acc = (
        jnp.einsum("rhqk,rkhd->rqhd", score_low, key_heads, preferred_element_type=f32) * scale
    )
    query_piece = lax.all_gather(
        queries.reshape(row_count, frame_count, width).astype(f32).astype(jnp.bfloat16),
        "seq",
        axis=1,
        tiled=True,
    ).astype(jnp.float32)
    grad_piece = lax.all_gather(
        attended_grad.reshape(row_count, frame_count, width).astype(f32).astype(jnp.bfloat16),
        "seq",
        axis=1,
        tiled=True,
    ).astype(jnp.float32)
    log_piece = lax.all_gather(
        log_total.transpose(0, 2, 1).astype(jnp.bfloat16), "seq", axis=1, tiled=True
    ).astype(jnp.float32)
    delta_piece = lax.all_gather(
        delta.transpose(0, 2, 1).astype(jnp.bfloat16), "seq", axis=1, tiled=True
    ).astype(jnp.float32)
    count = query_piece.shape[1]
    query_heads = query_piece.astype(bf16).reshape(row_count, count, head_count, head_size)
    grad_heads = grad_piece.astype(bf16).reshape(row_count, count, head_count, head_size)
    scores = (
        jnp.einsum("rqhd,rkhd->rhqk", query_heads, key_heads_own, preferred_element_type=f32)
        * scale
    )
    other_pos = jnp.arange(count, dtype=jnp.int32)
    causal = query_pos[None, None, :] <= other_pos[None, :, None]
    same_clip = segments[:, None, :] == all_segments[:, :, None]
    allowed = (causal & same_clip)[:, None]
    log_rows = log_piece.transpose(0, 2, 1)
    delta_rows = delta_piece.transpose(0, 2, 1)
    prob = jnp.where(allowed, jnp.exp(scores - log_rows[..., None]), 0.0)
    value_acc = jnp.einsum(
        "rhqk,rqhd->rkhd", prob.astype(bf16), grad_heads, preferred_element_type=f32
    )
    prob_part = jnp.einsum(
        "rqhd,rkhd->rhqk", grad_heads, value_heads_own, preferred_element_type=f32
    )
    score_low = (prob * (prob_part - delta_rows[..., None])).astype(bf16)
    key_acc = (
        jnp.einsum("rhqk,rqhd->rkhd", score_low, query_heads, preferred_element_type=f32) * scale
    )
    packed_grad = jnp.concatenate(
        [
            query_acc.reshape(token_count, width),
            key_acc.reshape(token_count, width),
            value_acc.reshape(token_count, width),
        ],
        axis=1,
    ).astype(bf16)
    qkv_grad = left_tmul(normed_one, packed_grad)
    normed_one_grad = right_tmul(packed_grad, qkv_back)
    input_res_grad, gain_one_grad, shift_one_grad = norm_back(
        inputs, gain_one_b.astype(f32), shift_one_b.astype(f32), normed_one_grad
    )
    frames_grad = (
        (after_self_grad + input_res_grad).astype(bf16).reshape(row_count, frame_count, width)
    )
    summed = (
        lax.psum_scatter(gain_one_grad, ("dp", "seq"), scatter_dimension=0, tiled=True),
        lax.psum_scatter(shift_one_grad, ("dp", "seq"), scatter_dimension=0, tiled=True),
        lax.psum_scatter(qkv_grad, ("dp", "seq"), scatter_dimension=0, tiled=True),
        lax.psum_scatter(out_grad, ("dp", "seq"), scatter_dimension=0, tiled=True),
        lax.psum_scatter(gain_two_grad, ("dp", "seq"), scatter_dimension=0, tiled=True),
        lax.psum_scatter(shift_two_grad, ("dp", "seq"), scatter_dimension=0, tiled=True),
        lax.psum_scatter(query_grad, ("dp", "seq"), scatter_dimension=0, tiled=True),
        lax.psum_scatter(project_grad, ("dp", "seq"), scatter_dimension=0, tiled=True),
        lax.psum_scatter(bias_grad, ("dp", "seq"), scatter_dimension=0, tiled=True),
        lax.psum_scatter(keyvalue_weight_grad, ("dp", "seq"), scatter_dimension=0, tiled=True),
        lax.psum_scatter(crossout_grad, ("dp", "seq"), scatter_dimension=0, tiled=True),
        lax.psum_scatter(gain_three_grad, ("dp", "seq"), scatter_dimension=0, tiled=True),
        lax.psum_scatter(shift_three_grad, ("dp", "seq"), scatter_dimension=0, tiled=True),
        lax.psum_scatter(feedin_grad, ("dp", "seq"), scatter_dimension=0, tiled=True),
        lax.psum_scatter(feedout_grad, ("dp", "seq"), scatter_dimension=0, tiled=True),
    )
    return (block_out, frames_grad, text_grad) + tuple(summed)


def solution(mesh):
    placed = (
        P("dp", "seq", None),
        P("dp", "seq"),
        P("dp", None, None, None),
        P("dp", None),
        P("dp", "seq", None),
        P(("dp", "seq")),
        P(("dp", "seq")),
        P(("dp", "seq"), None),
        P(("dp", "seq"), None),
        P(("dp", "seq")),
        P(("dp", "seq")),
        P(("dp", "seq"), None),
        P(("dp", "seq"), None),
        P(("dp", "seq")),
        P(("dp", "seq"), None),
        P(("dp", "seq"), None),
        P(("dp", "seq")),
        P(("dp", "seq")),
        P(("dp", "seq"), None),
        P(("dp", "seq"), None),
    )
    paired = mesh.shape["seq"] == 2 and mesh.shape["dp"] == 16
    return jax.shard_map(
        per_device_rows if paired else per_device,
        mesh=mesh,
        in_specs=placed,
        out_specs=(
            P("dp", "seq", None),
            P("dp", "seq", None),
            P("dp", None, "seq", None),
            P(("dp", "seq")),
            P(("dp", "seq")),
            P(("dp", "seq"), None),
            P(("dp", "seq"), None),
            P(("dp", "seq")),
            P(("dp", "seq")),
            P(("dp", "seq"), None),
            P(("dp", "seq"), None),
            P(("dp", "seq")),
            P(("dp", "seq"), None),
            P(("dp", "seq"), None),
            P(("dp", "seq")),
            P(("dp", "seq")),
            P(("dp", "seq"), None),
            P(("dp", "seq"), None),
        ),
        check_vma=False,
    )
```
